32 devices in a mesh: seq: 16 (over z, y, x), head: 2 (over core).
Axes of the slice: x: 2, y: 2, z: 4, core: 2. Of those that a mesh axis runs over, the one named last changes fastest.
Arguments:
- query_rows: bfloat16 [32, 4096, 128], P('head', 'seq'), may hold values from -6 to 6
- key_rows: bfloat16 [32, 4096, 128], P('head', 'seq'), may hold values from -0.5 to 0.5
- value_rows: bfloat16 [32, 4096, 128], P('head', 'seq'), may hold values from -40 to 40
- log_gate: float32 [32, 4096], P('head', 'seq'), may hold values from -1 to 0
- episode: int32 [4096], P('seq'), may hold values from 0 to 3, never falling along the last dimension, each value on 1 to 2048 neighbouring positions
- grad_out: bfloat16 [32, 4096, 128], P('head', 'seq'), may hold values from -6 to 6
Outputs:
- normed: bfloat16 [32, 4096, 128], P('head', 'seq')
- grad_query: bfloat16 [32, 4096, 128], P('head', 'seq')
- grad_key: bfloat16 [32, 4096, 128], P('head', 'seq')
- grad_value: bfloat16 [32, 4096, 128], P('head', 'seq')
The draws below stay inside these ranges and needn't reach their ends.
Inputs may be any that keep to these rules, and one draw needn't show every extreme that they name: Episode ids never fall along the tokens; every episode spans 1 to 2048 tokens and one spans exactly 2048.
All inputs are finite; a program needn't handle non-finite values.
Results may differ from the reference program's by a relative error of at most 0.0062.
Values sent between devices are 32-bit elements; how exact they have to be, the bound alone decides.
A program may use at most 64 MiB of HBM per device.

```python
import math
import jax
import jax.numpy as jnp
import numpy as np
from jax import lax

HEAD_DIM = 128
HEADS = 32
STRETCH = 256
TOK_DEV = 256
TOKENS = 4096
EP_MOST = 2048
EPISODES = 4


def draw_value_rows(key, part):
    noise_key, spread_key = jax.random.split(key, 2)
    position = jnp.arange(HEADS, dtype=jnp.float32)[:, None, None] / max(HEADS - 1, 1)
    ramped = jnp.exp(math.log(3.0) * (position - 0.5))
    spread = jnp.exp(math.log(10.0) * (jax.random.uniform(spread_key, (HEADS, 1, HEAD_DIM), jnp.float32) - 0.5))
    result = jax.random.normal(noise_key, (HEADS, TOKENS, HEAD_DIM), jnp.float32) * spread * ramped
    return jnp.clip(result, -40.0, 40.0).astype(jnp.bfloat16)


def draw_log_gate(key, part):
    fast_key, slow_key, quick_key, rough_key, block_key, location_seed, loss_key = jax.random.split(key, 7)
    fraction = 0.5
    fast = jax.random.bernoulli(fast_key, fraction, (HEADS, 1))
    slow_rate = jnp.exp(jax.random.uniform(slow_key, (HEADS, 1), jnp.float32, math.log(0.1), math.log(0.6))) / EP_MOST
    quick_rate = jnp.exp(jax.random.uniform(quick_key, (HEADS, 1), jnp.float32, math.log(1.0 / 50.0), math.log(1.0 / 30.0)))
    forgetting_factors = jnp.where(fast, quick_rate, slow_rate)
    perturbation_broad = jax.random.uniform(rough_key, (HEADS, TOKENS), jnp.float32, 0.5, 2.0)
    partition_sets = jnp.exp(jax.random.uniform(block_key, (HEADS, TOKENS // TOK_DEV), jnp.float32, math.log(0.6), math.log(1.7)))
    partition_sets = jnp.repeat(partition_sets, TOK_DEV, axis=1)
    spots = jax.random.randint(location_seed, (6,), 0, TOKENS)
    restart_markers = jnp.any(jnp.arange(TOKENS)[:, None] == spots[None, :], axis=1)
    objective_outputs = jax.random.uniform(loss_key, (HEADS, TOKENS), jnp.float32, math.log(0.5), math.log(0.8))
    episode_lengths = jnp.where(restart_markers[None, :], objective_outputs, 0.0)
    return (-forgetting_factors * perturbation_broad * partition_sets + episode_lengths).astype(jnp.float32)


def block_scale(rng, extent, shards, low, high):
    level = 1.0
    for dim, blocks in shards:
        steps = jax.random.uniform(jax.random.fold_in(jax.random.fold_in(rng, 6), dim), (blocks,), jnp.float32, low / len(shards), high / len(shards))
        level = level * jnp.repeat(jnp.exp(steps), extent[dim] // blocks).reshape((-1,) + (1,) * (len(extent) - 1 - dim))
    return level


def length_profile(count, total, limit, lean):
    weights = [(1 << 20) // math.isqrt(rank ** lean) + 1 for rank in range(2, count + 1)]
    spare, given = total - limit - (count - 1), [1] * (count - 1)
    while spare > 0:
        candidates = [i for i in range(count - 1) if given[i] < limit]
        whole, left = sum([weights[i] for i in candidates]), spare
        for i in candidates:
            addition = min(limit - given[i], max(1, left * weights[i] // whole), spare)
            given[i] = given[i] + addition
            spare = spare - addition
    return np.array([limit] + given)


def ragged(key, amount, total, bound, lean):
    if amount == 2:
        one = jax.random.randint(key, (), max(1, total - bound), min(bound, total - 1) + 1)
        return jnp.stack([one, total - one])
    sizes = jnp.asarray(length_profile(amount, total, bound, lean), jnp.int32)
    twos = (amount - 1) // 2
    donor, receiver = sizes[1:1 + 2 * twos:2], sizes[2:2 + 2 * twos:2]
    margin = jnp.minimum(donor - 1, bound - receiver)
    passed = jax.random.randint(jax.random.fold_in(key, 1), (twos,), 0, 1 << 20) % (margin + 1)
    sizes = sizes.at[1:1 + 2 * twos:2].set(donor - passed).at[2:2 + 2 * twos:2].set(receiver + passed)
    return sizes[jax.random.permutation(jax.random.fold_in(key, 2), amount)]


def normal_values(key, shape, scale, bound, pieces=(), held_as=jnp.bfloat16):
    array = jax.random.normal(key, shape, jnp.float32) * scale
    if len(pieces) > 0:
        array = block_scale(key, shape, pieces, -0.22, 0.18) * array
    return jnp.clip(array, min=-bound, max=bound).astype(held_as)


def setup_inputs(seed: int = 0) -> dict:
    splits = jax.random.split(jax.random.key(seed), 7)
    return {
        "query_rows": normal_values(splits[0], (HEADS, TOKENS, HEAD_DIM), 1.0, 6.0, ((0, 2), (1, 16))),
        "key_rows": normal_values(splits[1], (HEADS, TOKENS, HEAD_DIM), (HEAD_DIM ** -0.5), 0.5, ((0, 2), (1, 16))),
        "value_rows": draw_value_rows(jax.random.fold_in(splits[6], 71), 0),
        "log_gate": draw_log_gate(jax.random.fold_in(splits[6], 71), 0),
        "episode": jnp.searchsorted(jnp.cumsum(ragged(splits[4], EPISODES, TOKENS, EP_MOST, 2)), jnp.arange(TOKENS), side="right").astype(jnp.int32),
        "grad_out": normal_values(splits[5], (HEADS, TOKENS, HEAD_DIM), 1.0, 6.0, ((0, 2), (1, 16))),
    }


EPSILON = 1e-06

def rounded(values):
    return lax.optimization_barrier(values.astype(jnp.bfloat16)).astype(jnp.float32)

def stretch_terms(gates, episodes):
    running = jnp.cumsum(gates, axis=-1)
    length = episodes.shape[0]
    causal = jnp.arange(length)[:, None] >= jnp.arange(length)[None, :]
    allowed = ((episodes[:, None] == episodes[None, :]) & causal)[None]
    differences = running[:, :, None] - running[:, None, :]
    decays = jnp.where(allowed, jnp.exp(jnp.where(allowed, differences, 0.0)), 0.0)
    return (running, decays)

def reference(query_rows, key_rows, value_rows, log_gate, episode, grad_out):
    head_count, tokens, head_width = query_rows.shape
    stretch_count = tokens // STRETCH

    def split_stretches(values):
        return jnp.moveaxis(values.reshape(head_count, stretch_count, STRETCH, head_width), 1, 0)

    def join_stretches(values):
        return jnp.moveaxis(values, 0, 1).reshape(head_count, tokens, head_width)
    queries = split_stretches(query_rows)
    keyset = split_stretches(key_rows)
    values = split_stretches(value_rows)
    gates = jnp.moveaxis(log_gate.reshape(head_count, stretch_count, STRETCH), 1, 0)
    episodes = episode.reshape(stretch_count, STRETCH)

    def forward_stretch(carried_in, inputs):
        state, previous = carried_in
        stretch_query, stretch_key, stretch_value, stretch_gate, stretch_episode = inputs
        running, decays = stretch_terms(stretch_gate, stretch_episode)
        query_wide = stretch_query.astype(jnp.float32)
        key_wide = stretch_key.astype(jnp.float32)
        value_wide = stretch_value.astype(jnp.float32)
        scores = rounded(jnp.einsum('hcd,hsd->hcs', query_wide, key_wide) * decays)
        within = jnp.einsum('hcs,hse->hce', scores, value_wide)
        state_low = rounded(state)
        carried = jnp.where((stretch_episode == previous)[None, :], jnp.exp(running), 0.0)
        attention = within + jnp.einsum('hcd,hde->hce', query_wide, state_low) * carried[:, :, None]
        last_id = stretch_episode[-1]
        weight = jnp.where((stretch_episode == last_id)[None, :], jnp.exp(running[:, -1:] - running), 0.0)
        keys_decayed = rounded(key_wide * weight[:, :, None])
        local_state = jnp.einsum('hcd,hce->hde', keys_decayed, value_wide)
        kept = jnp.where(previous == last_id, jnp.exp(running[:, -1])[:, None, None] * state, 0.0)
        return ((kept + local_state, last_id), (attention, state_low, previous))
    start = (jnp.zeros((head_count, head_width, head_width), jnp.float32), jnp.int32(-1))
    ignored, (attention_all, state_lows, previous_ids) = lax.scan(forward_stretch, start, (queries, keyset, values, gates, episodes))
    attention = join_stretches(attention_all)
    cotangent = grad_out.astype(jnp.float32)
    features = head_count * head_width
    squared_terms = lax.optimization_barrier(jnp.sum(attention * attention, axis=(0, 2)))
    crossed = lax.optimization_barrier(jnp.sum(cotangent * attention, axis=(0, 2)))
    root_mean = jnp.sqrt(squared_terms / features + EPSILON)
    normed = (attention / root_mean[None, :, None]).astype(jnp.bfloat16)
    grad_attn = ((cotangent - attention * (crossed / (features * root_mean * root_mean))[None, :, None]) / root_mean[None, :, None]).astype(jnp.bfloat16)
    grad_stretches = split_stretches(grad_attn)

    def backward_stretch(carried_in, inputs):
        back, following = carried_in
        stretch_query, stretch_key, stretch_value, stretch_gate, stretch_episode, stretch_grad, state_low, previous = inputs
        running, decays = stretch_terms(stretch_gate, stretch_episode)
        query_wide = stretch_query.astype(jnp.float32)
        key_wide = stretch_key.astype(jnp.float32)
        value_wide = stretch_value.astype(jnp.float32)
        grad_wide = stretch_grad.astype(jnp.float32)
        scores = rounded(jnp.einsum('hcd,hsd->hcs', query_wide, key_wide) * decays)
        score_gradient = rounded(jnp.einsum('hce,hse->hcs', grad_wide, value_wide) * decays)
        carried = jnp.where((stretch_episode == previous)[None, :], jnp.exp(running), 0.0)
        query_grad = jnp.einsum('hcs,hsd->hcd', score_gradient, key_wide) + jnp.einsum('hce,hde->hcd', grad_wide, state_low) * carried[:, :, None]
        back_low = rounded(back)
        trailing = jnp.where((stretch_episode == following)[None, :], jnp.exp(running[:, -1:] - running), 0.0)
        key_grad = jnp.einsum('hcs,hcd->hsd', score_gradient, query_wide) + jnp.einsum('hce,hde->hcd', value_wide, back_low) * trailing[:, :, None]
        value_grad = jnp.einsum('hcs,hce->hse', scores, grad_wide) + jnp.einsum('hcd,hde->hce', key_wide, back_low) * trailing[:, :, None]
        first_id = stretch_episode[0]
        query_weight = jnp.where((stretch_episode == first_id)[None, :], jnp.exp(running), 0.0)
        queries_decayed = rounded(query_wide * query_weight[:, :, None])
        local_back = jnp.einsum('hcd,hce->hde', queries_decayed, grad_wide)
        kept = jnp.where(first_id == following, jnp.exp(running[:, -1])[:, None, None] * back, 0.0)
        outputs = (query_grad.astype(jnp.bfloat16), key_grad.astype(jnp.bfloat16), value_grad.astype(jnp.bfloat16))
        return ((kept + local_back, first_id), outputs)
    ignored_back, (query_grads, key_grads, value_grads) = lax.scan(backward_stretch, start, (queries, keyset, values, gates, episodes, grad_stretches, state_lows, previous_ids), reverse=True)
    return (normed, join_stretches(query_grads), join_stretches(key_grads), join_stretches(value_grads))
```

```python
import functools

import jax
import jax.numpy as jnp
from jax import lax
from jax.experimental import pallas as pl
from jax.experimental.pallas import tpu as pltpu
from jax.sharding import PartitionSpec as P

EPSILON = 1e-06
GROUP = 4
BLOCKED = -1e30
MIB = 1 << 20
F32 = jnp.float32
BF16 = jnp.bfloat16
MESH = pl.DeviceIdType.MESH


def product(a, b, over_a, over_b):
    return lax.dot_general(a, b, (((over_a,), (over_b,)), ((), ())), preferred_element_type=F32)


def kernel(
    nseq, nhead, features,
    q_ref, k_ref, v_ref, gate_ref, ep_ref, go_ref,
    normed_ref, gq_ref, gk_ref, gv_ref,
    run_ref, runc_ref, grow_ref, fall_ref, keep_ref, allow_ref, epc_ref, decay_ref, score_ref,
    att_ref, gattn_ref, kin_ref, vin_ref, sums_ref, stat_ref, other_ref, norm_ref, corr_ref,
    ids_ref, prev_ref, next_ref,
    local_ref, group_ref, chain_ref, leave_ref, enter_ref, state_ref,
    blocal_ref, bgroup_ref, bchain_ref, bleave_ref, benter_ref, bstate_ref,
    id_send, id_recv, stat_send, stat_recv,
    up_send, up_recv, chain_send, chain_recv, down_send, down_recv,
    bup_send, bup_recv, bchain_send, bchain_recv, bdown_send, bdown_recv,
):
    heads, tokens, width = q_ref.shape
    owned = heads // GROUP
    groups = nseq // GROUP
    s = lax.axis_index("seq")
    hd = lax.axis_index("head")
    c = lax.rem(s, GROUP)
    z = s // GROUP
    base = s - c

    def member(position):
        return {"seq": base + position}

    def other(distance):
        return lax.rem(c + distance, GROUP)

    barrier = pltpu.get_barrier_semaphore()

    def greet(device):
        pl.semaphore_signal(barrier, inc=1, device_id=device, device_id_type=MESH)

    for d in range(1, GROUP):
        greet(member(other(d)))
    for d in range(1, nhead):
        greet({"head": lax.rem(hd + d, nhead)})

    @pl.when(s > 0)
    def _():
        greet({"seq": s - 1})

    @pl.when(s < nseq - 1)
    def _():
        greet({"seq": s + 1})

    @pl.when(z > 0)
    def _():
        greet({"seq": s - GROUP})

    @pl.when(z < groups - 1)
    def _():
        greet({"seq": s + GROUP})

    lane = lax.broadcasted_iota(jnp.int32, gate_ref.shape, 1)
    run = gate_ref[...]
    step = 1
    while step < tokens:
        run = run + jnp.where(lane >= step, pltpu.roll(run, step, 1), 0.0)
        step *= 2
    run_ref[...] = run
    total = run[:, tokens - 1 : tokens]
    columns = run.T
    grown = jnp.exp(run).T
    fallen = jnp.exp(total - run).T
    for h in range(heads):
        runc_ref[h] = jnp.broadcast_to(columns[:, h : h + 1], (tokens, width))
        grow_ref[h] = jnp.broadcast_to(grown[:, h : h + 1], (tokens, width))
        fall_ref[h] = jnp.broadcast_to(fallen[:, h : h + 1], (tokens, width))
    ep_row = ep_ref[...].astype(F32)
    ep_col = jnp.broadcast_to(jnp.broadcast_to(ep_row, (8, tokens)).T[:, 0:1], (tokens, width))
    epc_ref[...] = ep_col
    first_id = ep_row[:, 0:1]
    last_id = ep_row[:, tokens - 1 : tokens]
    wide = jnp.concatenate([ep_col] * (tokens // width), axis=1)
    below = lax.broadcasted_iota(jnp.int32, (tokens, tokens), 0) >= lax.broadcasted_iota(
        jnp.int32, (tokens, tokens), 1
    )
    allow_ref[...] = jnp.where(below & (wide == ep_row), 0.0, BLOCKED)
    half = lax.broadcasted_iota(jnp.int32, (8, width), 1) < width // 2
    ids_ref[...] = jnp.where(half, first_id, last_id)

    beside = jnp.minimum(s, 1) + jnp.minimum(nseq - 1 - s, 1)
    across = jnp.minimum(z, 1) + jnp.minimum(groups - 1 - z, 1)
    pl.semaphore_wait(barrier, GROUP - 1 + nhead - 1 + beside + across)

    def remote(src, dst, send, recv, device):
        return pltpu.make_async_remote_copy(
            src_ref=src, dst_ref=dst, send_sem=send, recv_sem=recv, device_id=device, device_id_type=MESH
        )

    def ids_after():
        return remote(ids_ref, prev_ref, id_send.at[0], id_recv.at[0], {"seq": s + 1})

    def ids_before():
        return remote(ids_ref, next_ref, id_send.at[1], id_recv.at[1], {"seq": s - 1})

    @pl.when(s < nseq - 1)
    def _():
        ids_after().start()

    @pl.when(s > 0)
    def _():
        ids_before().start()

    @pl.when(s == 0)
    def _():
        prev_ref[...] = jnp.full_like(prev_ref, -1.0)

    @pl.when(s == nseq - 1)
    def _():
        next_ref[...] = jnp.full_like(next_ref, -1.0)

    @pl.when(s < nseq - 1)
    def _():
        ids_after().wait_send()
        ids_before().wait_recv()

    @pl.when(s > 0)
    def _():
        ids_before().wait_send()
        ids_after().wait_recv()

    prev_id = prev_ref[0:1, width - 1 : width]
    next_id = next_ref[0:1, 0:1]
    passed = jnp.broadcast_to(jnp.exp(total), (total.shape[0], width))
    keep_ref[0] = jnp.where(prev_id == last_id, passed, 0.0)
    keep_ref[1] = jnp.where(next_id == first_id, passed, 0.0)

    def up_copy(local, group, send, recv, position, i):
        return remote(
            local.at[position * owned + i], group.at[c, i], send.at[position, i], recv.at[c, i], member(position)
        )

    def up_wait(local, group, send, recv, position, i):
        remote(
            local.at[position * owned + i], group.at[position, i], send.at[position, i], recv.at[position, i],
            member(position),
        ).wait()

    def down_copy(leave, state, send, recv, position, i):
        return remote(
            leave.at[position, i], state.at[c * owned + i], send.at[position, i], recv.at[c, i], member(position)
        )

    def down_wait(leave, state, send, recv, position, i):
        remote(
            leave.at[position, i], state.at[position * owned + i], send.at[position, i], recv.at[position, i],
            member(position),
        ).wait()

    def local_states(i, _):
        for d in (1, 2, 3, 0):
            position = other(d)
            h = position * owned + i
            weight = jnp.where(epc_ref[...] == last_id, fall_ref[h], 0.0)
            decayed = (k_ref[h].astype(F32) * weight).astype(BF16)
            value = product(decayed, v_ref[h], 0, 0)
            factor = jnp.broadcast_to(keep_ref[0, pl.ds(h, 1), :], (8, width))
            if d == 0:
                group_ref[c, i, 0:width] = value
                group_ref[c, i, width:] = factor
            else:
                local_ref[h, 0:width] = value
                local_ref[h, width:] = factor
                up_copy(local_ref, group_ref, up_send, up_recv, position, i).start()
        return 0

    lax.fori_loop(0, owned, local_states, 0)

    def scan_owned(i, order, begin, has_before, has_after, local, group, chain, leave, enter, state, sems, step):
        usend, urecv, csend, crecv, dsend, drecv = sems

        for d in range(1, GROUP):
            up_wait(local, group, usend, urecv, other(d), i)

        def onward():
            return remote(enter.at[i], chain.at[i], csend.at[i], crecv.at[i], {"seq": s + step})

        def arrival():
            return remote(enter.at[i], chain.at[i], csend.at[i], crecv.at[i], {"seq": s - step})

        inner = None
        factors = None
        for j in order:
            leave_factor = group[j, i, width : width + 1, :]
            if inner is None:
                inner = group[j, i, 0:width]
                factors = leave_factor
            else:
                inner = inner * leave_factor + group[j, i, 0:width]
                factors = factors * leave_factor

        @pl.when(has_before)
        def _():
            arrival().wait_recv()

        @pl.when(jnp.logical_not(has_before))
        def _():
            chain[i] = jnp.zeros((width, width), F32)

        enter[i] = inner + factors * chain[i]

        @pl.when(has_after)
        def _():
            onward().start()

        carried = chain[i]
        for j in order:
            leave[j, i] = carried
            carried = carried * group[j, i, width : width + 1, :] + group[j, i, 0:width]
        for d in range(1, GROUP):
            down_copy(leave, state, dsend, drecv, other(d), i).start()
        state[c * owned + i] = leave[c, i]

        @pl.when(has_after)
        def _():
            onward().wait_send()

    def forward_part(i, _):
        for position in range(GROUP):
            h = position * owned + i
            runc = jnp.concatenate([runc_ref[h]] * (tokens // width), axis=1)
            decay = jnp.exp(runc - run_ref[pl.ds(h, 1), :] + allow_ref[...])
            decay_ref[h] = decay
            score = (product(q_ref[h], k_ref[h], 1, 1) * decay).astype(BF16)
            score_ref[h] = score
            att_ref[h] = product(score, v_ref[h], 1, 0)
        scan_owned(
            i, range(GROUP), 0, z > 0, z < groups - 1,
            local_ref, group_ref, chain_ref, leave_ref, enter_ref, state_ref,
            (up_send, up_recv, chain_send, chain_recv, down_send, down_recv), GROUP,
        )
        return 0

    lax.fori_loop(0, owned, forward_part, 0)

    sums_ref[...] = jnp.zeros_like(sums_ref)

    def attend(i, _):
        for d in range(1, GROUP):
            down_wait(leave_ref, state_ref, down_send, down_recv, other(d), i)
        squares = sums_ref[0]
        crosses = sums_ref[1]
        for position in range(GROUP):
            h = position * owned + i
            carried = jnp.where(epc_ref[...] == prev_id, grow_ref[h], 0.0)
            low = state_ref[h].astype(BF16)
            att = att_ref[h] + product(q_ref[h], low, 1, 0) * carried
            att_ref[h] = att
            squares = squares + att * att
            crosses = crosses + go_ref[h].astype(F32) * att
        sums_ref[0] = squares
        sums_ref[1] = crosses
        return 0

    lax.fori_loop(0, owned, attend, 0)
    square = jnp.sum(sums_ref[0], axis=1, keepdims=True)
    cross = jnp.sum(sums_ref[1], axis=1, keepdims=True)
    first_half = lax.broadcasted_iota(jnp.int32, (tokens, width), 1) < width // 2
    stat_ref[...] = jnp.where(first_half, square, cross)

    def stat_copy(d, slot):
        return remote(
            stat_ref, other_ref.at[slot], stat_send.at[d - 1], stat_recv.at[slot], {"head": lax.rem(hd + d, nhead)}
        )

    for d in range(1, nhead):
        stat_copy(d, d - 1).start()
    for d in range(1, nhead):
        stat_copy(d, d - 1).wait()
    summed = stat_ref[...]
    for d in range(1, nhead):
        summed = summed + other_ref[d - 1]
    square = summed[:, 0:1]
    cross = summed[:, width // 2 : width // 2 + 1]
    mean_square = square / features + EPSILON
    inverse = lax.rsqrt(mean_square)
    norm_ref[...] = jnp.broadcast_to(inverse, (tokens, width))
    corr_ref[...] = jnp.broadcast_to(cross / (features * mean_square), (tokens, width))

    def back_local(i, _):
        for d in (1, 2, 3, 0):
            position = other(d)
            h = position * owned + i
            att = att_ref[h]
            normed_ref[h] = (att * norm_ref[...]).astype(BF16)
            grad = ((go_ref[h].astype(F32) - att * corr_ref[...]) * norm_ref[...]).astype(BF16)
            gattn_ref[h] = grad
            weight = jnp.where(epc_ref[...] == first_id, grow_ref[h], 0.0)
            decayed = (q_ref[h].astype(F32) * weight).astype(BF16)
            value = product(decayed, grad, 0, 0)
            factor = jnp.broadcast_to(keep_ref[1, pl.ds(h, 1), :], (8, width))
            if d == 0:
                bgroup_ref[c, i, 0:width] = value
                bgroup_ref[c, i, width:] = factor
            else:
                blocal_ref[h, 0:width] = value
                blocal_ref[h, width:] = factor
                up_copy(blocal_ref, bgroup_ref, bup_send, bup_recv, position, i).start()
        return 0

    lax.fori_loop(0, owned, back_local, 0)

    def backward_part(i, _):
        for position in range(GROUP):
            h = position * owned + i
            grad = gattn_ref[h]
            grad_score = (product(grad, v_ref[h], 1, 1) * decay_ref[h]).astype(BF16)
            carried = jnp.where(epc_ref[...] == prev_id, grow_ref[h], 0.0)
            low = state_ref[h].astype(BF16)
            gq_ref[h] = (
                product(grad_score, k_ref[h], 1, 0) + product(grad, low, 1, 1) * carried
            ).astype(BF16)
            kin_ref[h] = product(grad_score, q_ref[h], 0, 0)
            vin_ref[h] = product(score_ref[h], grad, 0, 0)
        scan_owned(
            i, range(GROUP - 1, -1, -1), 0, z < groups - 1, z > 0,
            blocal_ref, bgroup_ref, bchain_ref, bleave_ref, benter_ref, bstate_ref,
            (bup_send, bup_recv, bchain_send, bchain_recv, bdown_send, bdown_recv), -GROUP,
        )
        return 0

    lax.fori_loop(0, owned, backward_part, 0)

    def finish(i, _):
        for d in range(1, GROUP):
            down_wait(bleave_ref, bstate_ref, bdown_send, bdown_recv, other(d), i)
        for position in range(GROUP):
            h = position * owned + i
            trailing = jnp.where(epc_ref[...] == next_id, fall_ref[h], 0.0)
            low = bstate_ref[h].astype(BF16)
            gk_ref[h] = (kin_ref[h] + product(v_ref[h], low, 1, 1) * trailing).astype(BF16)
            gv_ref[h] = (vin_ref[h] + product(k_ref[h], low, 1, 0) * trailing).astype(BF16)
        return 0

    lax.fori_loop(0, owned, finish, 0)


def per_device(nseq, nhead, query_rows, key_rows, value_rows, log_gate, episode, grad_out):
    heads, tokens, width = query_rows.shape
    owned = heads // GROUP
    padded = -(-heads // 8) * 8
    if padded != heads:
        log_gate = jnp.pad(log_gate, ((0, padded - heads), (0, 0)))
    vmem = pl.BlockSpec(memory_space=pltpu.VMEM)
    rows = jax.ShapeDtypeStruct(query_rows.shape, BF16)
    block = (heads, tokens, width)
    state_set = [
        pltpu.VMEM((heads, width + 8, width), F32),
        pltpu.VMEM((GROUP, owned, width + 8, width), F32),
        pltpu.VMEM((owned, width, width), F32),
        pltpu.VMEM((GROUP, owned, width, width), F32),
        pltpu.VMEM((owned, width, width), F32),
        pltpu.VMEM((heads, width, width), F32),
    ]
    sem_set = [
        pltpu.SemaphoreType.DMA((GROUP, owned)),
        pltpu.SemaphoreType.DMA((GROUP, owned)),
        pltpu.SemaphoreType.DMA((owned,)),
        pltpu.SemaphoreType.DMA((owned,)),
        pltpu.SemaphoreType.DMA((GROUP, owned)),
        pltpu.SemaphoreType.DMA((GROUP, owned)),
    ]
    others = max(nhead - 1, 1)
    return pl.pallas_call(
        functools.partial(kernel, nseq, nhead, float(heads * nhead * width)),
        out_shape=[rows] * 4,
        in_specs=[vmem] * 6,
        out_specs=[vmem] * 4,
        scratch_shapes=[
            pltpu.VMEM((padded, tokens), F32),
            pltpu.VMEM(block, F32),
            pltpu.VMEM(block, F32),
            pltpu.VMEM(block, F32),
            pltpu.VMEM((2, padded, width), F32),
            pltpu.VMEM((tokens, tokens), F32),
            pltpu.VMEM((tokens, width), F32),
            pltpu.VMEM((heads, tokens, tokens), F32),
            pltpu.VMEM((heads, tokens, tokens), BF16),
            pltpu.VMEM(block, F32),
            pltpu.VMEM(block, BF16),
            pltpu.VMEM(block, F32),
            pltpu.VMEM(block, F32),
            pltpu.VMEM((2, tokens, width), F32),
            pltpu.VMEM((tokens, width), F32),
            pltpu.VMEM((others, tokens, width), F32),
            pltpu.VMEM((tokens, width), F32),
            pltpu.VMEM((tokens, width), F32),
            pltpu.VMEM((8, width), F32),
            pltpu.VMEM((8, width), F32),
            pltpu.VMEM((8, width), F32),
            *state_set,
            *state_set,
            pltpu.SemaphoreType.DMA((2,)),
            pltpu.SemaphoreType.DMA((2,)),
            pltpu.SemaphoreType.DMA((others,)),
            pltpu.SemaphoreType.DMA((others,)),
            *sem_set,
            *sem_set,
        ],
        compiler_params=pltpu.CompilerParams(
            collective_id=0, has_side_effects=True, vmem_limit_bytes=56 * MIB
        ),
        cost_estimate=pl.CostEstimate(
            flops=heads * tokens * tokens * width * 18, bytes_accessed=heads * tokens * width * 16,
            transcendentals=heads * tokens * tokens,
        ),
    )(query_rows, key_rows, value_rows, log_gate, episode.reshape(1, tokens), grad_out)


def solution(mesh):
    rows = P("head", "seq", None)
    return jax.shard_map(
        functools.partial(per_device, mesh.shape["seq"], mesh.shape["head"]),
        mesh=mesh,
        in_specs=(rows, rows, rows, P("head", "seq"), P("seq"), rows),
        out_specs=(rows, rows, rows, rows),
        check_vma=False,
    )
```

```python
import functools

import jax
import jax.numpy as jnp
from jax import lax
from jax.experimental import pallas as pl
from jax.experimental.pallas import tpu as pltpu
from jax.sharding import PartitionSpec as P

EPSILON = 1e-06
GROUP = 4
REACH_MAX = 16
BLOCKED = -1e30
MIB = 1 << 20
F32 = jnp.float32
BF16 = jnp.bfloat16
MESH = pl.DeviceIdType.MESH


def product(a, b, over_a, over_b):
    return lax.dot_general(a, b, (((over_a,), (over_b,)), ((), ())), preferred_element_type=F32)


def kernel(
    nseq, nhead, features,
    q_in, k_in, v_in, gate_ref, ep_ref, go_in,
    normed_out, gq_out, gk_out, gv_out,
    q_ref, k_ref, v_ref, go_ref, normed_ref, gq_ref, gk_ref, gv_ref,
    run_ref, runc_ref, grow_ref, fall_ref, pass_ref, allow_ref, epc_ref, decay_ref, score_ref,
    att_ref, gattn_ref, kin_ref, vin_ref, sums_ref, stat_ref, other_ref, norm_ref, corr_ref,
    ids_ref, prev_ref, next_ref,
    local_ref, group_ref, chain_ref, leave_ref, enter_ref, state_ref,
    blocal_ref, bgroup_ref, bchain_ref, bleave_ref, benter_ref, bstate_ref,
    in_sem, out_sem, gk_sem, gv_sem, id_send, id_recv, stat_send, stat_recv,
    up_send, up_recv, chain_send, chain_recv, down_send, down_recv,
    bup_send, bup_recv, bchain_send, bchain_recv, bdown_send, bdown_recv,
):
    heads, tokens, width = q_ref.shape
    owned = heads // GROUP
    groups = nseq // GROUP
    reach = chain_ref.shape[0]
    s = lax.axis_index("seq")
    hd = lax.axis_index("head")
    c = lax.rem(s, GROUP)
    z = s // GROUP
    base = s - c

    def member(position):
        return {"seq": base + position}

    def other(distance):
        return lax.rem(c + distance, GROUP)

    loads = [
        pltpu.make_async_copy(src, dst, in_sem.at[n])
        for n, (src, dst) in enumerate(((k_in, k_ref), (v_in, v_ref), (q_in, q_ref), (go_in, go_ref)))
    ]
    for load in loads:
        load.start()

    barrier = pltpu.get_barrier_semaphore()

    def greet(device):
        pl.semaphore_signal(barrier, inc=1, device_id=device, device_id_type=MESH)

    for d in range(1, GROUP):
        greet(member(other(d)))
    for d in range(1, nhead):
        greet({"head": lax.rem(hd + d, nhead)})

    @pl.when(s > 0)
    def _():
        greet({"seq": s - 1})

    @pl.when(s < nseq - 1)
    def _():
        greet({"seq": s + 1})

    for d in range(1, reach + 1):

        @pl.when(z >= d)
        def _():
            greet({"seq": s - GROUP * d})

        @pl.when(z < groups - d)
        def _():
            greet({"seq": s + GROUP * d})

    lane = lax.broadcasted_iota(jnp.int32, gate_ref.shape, 1)
    run = gate_ref[...]
    step = 1
    while step < tokens:
        run = run + jnp.where(lane >= step, pltpu.roll(run, step, 1), 0.0)
        step *= 2
    run_ref[...] = run
    total = run[:, tokens - 1 : tokens]
    fallen = jnp.exp(total - run).T
    for h in range(heads):
        fall_ref[h] = jnp.broadcast_to(fallen[:, h : h + 1], (tokens, width))
    pass_ref[...] = jnp.broadcast_to(jnp.exp(total), (total.shape[0], width))
    ep_row = ep_ref[...].astype(F32)
    ep_col = jnp.broadcast_to(jnp.broadcast_to(ep_row, (8, tokens)).T[:, 0:1], (tokens, width))
    epc_ref[...] = ep_col
    first_id = ep_row[:, 0:1]
    last_id = ep_row[:, tokens - 1 : tokens]
    half = lax.broadcasted_iota(jnp.int32, (8, width), 1) < width // 2
    ids_ref[...] = jnp.where(half, first_id, last_id)
    row = lax.broadcasted_iota(jnp.int32, (8, width), 0)
    id_rows = jnp.where(row == 1, last_id, first_id)
    loads[0].wait()
    loads[1].wait()

    def local_state(i, position, target, at):
        h = position * owned + i
        weight = jnp.where(epc_ref[...] == last_id, fall_ref[h], 0.0)
        decayed = (k_ref[h].astype(F32) * weight).astype(BF16)
        target[*at, 0:width] = product(decayed, v_ref[h], 0, 0)
        target[*at, width:] = jnp.where(row == 0, pass_ref[pl.ds(h, 1), :], id_rows)

    def local_states(i):
        for d in (1, 2, 3):
            local_state(i, other(d), local_ref, (other(d) * owned + i,))
        local_state(i, c, group_ref, (c, i))

    local_states(0)

    beside = jnp.minimum(s, 1) + jnp.minimum(nseq - 1 - s, 1)
    across = jnp.minimum(z, reach) + jnp.minimum(groups - 1 - z, reach)
    pl.semaphore_wait(barrier, GROUP - 1 + nhead - 1 + beside + across)

    def remote(src, dst, send, recv, device):
        return pltpu.make_async_remote_copy(
            src_ref=src, dst_ref=dst, send_sem=send, recv_sem=recv, device_id=device, device_id_type=MESH
        )

    def ids_after():
        return remote(ids_ref, prev_ref, id_send.at[0], id_recv.at[0], {"seq": s + 1})

    def ids_before():
        return remote(ids_ref, next_ref, id_send.at[1], id_recv.at[1], {"seq": s - 1})

    def up_copy(local, group, send, recv, position, i):
        return remote(
            local.at[position * owned + i], group.at[c, i], send.at[position, i], recv.at[c, i], member(position)
        )

    def up_arrival(local, group, send, recv, position, i):
        return remote(
            local.at[position * owned + i], group.at[position, i], send.at[position, i], recv.at[position, i],
            member(position),
        )

    def down_copy(leave, state, send, recv, position, i):
        return remote(
            leave.at[position, i], state.at[c * owned + i], send.at[position, i], recv.at[c, i], member(position)
        )

    def down_arrival(leave, state, send, recv, position, i):
        return remote(
            leave.at[position, i], state.at[position * owned + i], send.at[position, i], recv.at[position, i],
            member(position),
        )

    forward_set = (
        local_ref, group_ref, chain_ref, leave_ref, enter_ref, state_ref,
        up_send, up_recv, chain_send, chain_recv, down_send, down_recv,
    )
    backward_set = (
        blocal_ref, bgroup_ref, bchain_ref, bleave_ref, benter_ref, bstate_ref,
        bup_send, bup_recv, bchain_send, bchain_recv, bdown_send, bdown_recv,
    )

    def send_local(i, buffers):
        local, group, _, _, _, _, usend, urecv = buffers[:8]
        for d in (1, 2, 3):
            up_copy(local, group, usend, urecv, other(d), i).start()

    send_local(0, forward_set)

    @pl.when(s < nseq - 1)
    def _():
        ids_after().start()

    @pl.when(s > 0)
    def _():
        ids_before().start()

    def more_states(i, _):
        local_states(i)
        send_local(i, forward_set)
        return 0

    lax.fori_loop(1, owned, more_states, 0)

    columns = run.T
    grown = jnp.exp(run).T
    for h in range(heads):
        runc_ref[h] = jnp.broadcast_to(columns[:, h : h + 1], (tokens, width))
        grow_ref[h] = jnp.broadcast_to(grown[:, h : h + 1], (tokens, width))
    wide = jnp.concatenate([epc_ref[...]] * (tokens // width), axis=1)
    below = lax.broadcasted_iota(jnp.int32, (tokens, tokens), 0) >= lax.broadcasted_iota(
        jnp.int32, (tokens, tokens), 1
    )
    allow_ref[...] = jnp.where(below & (wide == ep_row), 0.0, BLOCKED)

    def chain_copy(buffers, i, distance, sign):
        _, _, chain, _, enter, _, _, _, csend, crecv, _, _ = buffers
        return remote(
            enter.at[i], chain.at[distance - 1, i], csend.at[distance - 1, i], crecv.at[distance - 1, i],
            {"seq": s + sign * GROUP * distance},
        )

    def exists(distance, sign):
        return z < groups - distance if sign > 0 else z >= distance

    def send_total(i, sign, buffers):
        local, group, chain, leave, enter, state, usend, urecv, csend, crecv, dsend, drecv = buffers
        id_row = width + 1 if sign > 0 else width + 2
        for d in range(1, GROUP):
            up_arrival(local, group, usend, urecv, other(d), i).wait_recv()
        total_state = None
        for j in range(GROUP)[::sign]:
            factor = group[j, i, width : width + 1, :]
            mark = group[j, i, id_row : id_row + 1, :]
            if total_state is None:
                total_state = group[j, i, 0:width]
                factors = factor
            else:
                total_state = total_state * jnp.where(mark == before, factor, 0.0) + group[j, i, 0:width]
                factors = factors * factor
            before = mark
        enter[i, 0:width] = total_state
        enter[i, width:] = jnp.where(row == 0, factors, before)
        for d in range(1, reach + 1):

            @pl.when(exists(d, sign))
            def _():
                chain_copy(buffers, i, d, sign).start()

    def send_entering(i, sign, buffers):
        local, group, chain, leave, enter, state, usend, urecv, csend, crecv, dsend, drecv = buffers
        id_row = width + 1 if sign > 0 else width + 2
        for d in range(1, reach + 1):

            @pl.when(exists(d, -sign))
            def _():
                chain_copy(buffers, i, d, -sign).wait_recv()

            @pl.when(jnp.logical_not(exists(d, -sign)))
            def _():
                chain[d - 1, i] = jnp.zeros((width + 8, width), F32)

        carried = chain[reach - 1, i, 0:width]
        before = chain[reach - 1, i, width + 1 : width + 2, :]
        for d in range(reach - 1, 0, -1):
            mark = chain[d - 1, i, width + 1 : width + 2, :]
            factor = jnp.where(mark == before, chain[d - 1, i, width : width + 1, :], 0.0)
            carried = carried * factor + chain[d - 1, i, 0:width]
            before = mark
        for n, j in enumerate(range(GROUP)[::sign]):
            leave[j, i] = carried
            if n < GROUP - 1:
                mark = group[j, i, id_row : id_row + 1, :]
                factor = jnp.where(mark == before, group[j, i, width : width + 1, :], 0.0)
                carried = carried * factor + group[j, i, 0:width]
                before = mark
        for d in range(1, GROUP):
            down_copy(leave, state, dsend, drecv, other(d), i).start()
        state[c * owned + i] = leave[c, i]

    def state_arrival(i, buffers):
        _, _, _, leave, _, state, _, _, _, _, dsend, drecv = buffers
        for d in range(1, GROUP):
            down_arrival(leave, state, dsend, drecv, other(d), i).wait_recv()

    def settle(i, sign, buffers):
        local, group, _, leave, _, state, usend, urecv, _, _, dsend, drecv = buffers
        for d in range(1, GROUP):
            up_arrival(local, group, usend, urecv, other(d), i).wait_send()
            down_arrival(leave, state, dsend, drecv, other(d), i).wait_send()
        for d in range(1, reach + 1):

            @pl.when(exists(d, sign))
            def _():
                chain_copy(buffers, i, d, sign).wait_send()

    def scan(sign, buffers, part):
        part(0)

        def steps(i, _):
            send_total(i, sign, buffers)

            @pl.when(i < owned - 1)
            def _():
                part(i + 1)

            send_entering(i, sign, buffers)
            return 0

        lax.fori_loop(0, owned, steps, 0)

    def forward_part(i):
        for position in range(GROUP):
            h = position * owned + i
            runc = jnp.concatenate([runc_ref[h]] * (tokens // width), axis=1)
            decay = jnp.exp(runc - run_ref[pl.ds(h, 1), :] + allow_ref[...])
            decay_ref[h] = decay
            score = (product(q_ref[h], k_ref[h], 1, 1) * decay).astype(BF16)
            score_ref[h] = score
            att_ref[h] = product(score, v_ref[h], 1, 0)

    loads[2].wait()
    scan(1, forward_set, forward_part)

    @pl.when(s == 0)
    def _():
        prev_ref[...] = jnp.full_like(prev_ref, -1.0)

    @pl.when(s == nseq - 1)
    def _():
        next_ref[...] = jnp.full_like(next_ref, -1.0)

    @pl.when(s < nseq - 1)
    def _():
        ids_after().wait_send()
        ids_before().wait_recv()

    @pl.when(s > 0)
    def _():
        ids_before().wait_send()
        ids_after().wait_recv()

    prev_id = prev_ref[0:1, width - 1 : width]
    next_id = next_ref[0:1, 0:1]
    loads[3].wait()

    sums_ref[...] = jnp.zeros_like(sums_ref)

    def attend(i, _):
        state_arrival(i, forward_set)
        squares = sums_ref[0]
        crosses = sums_ref[1]
        for position in range(GROUP):
            h = position * owned + i
            carried = jnp.where(epc_ref[...] == prev_id, grow_ref[h], 0.0)
            low = state_ref[h].astype(BF16)
            att = att_ref[h] + product(q_ref[h], low, 1, 0) * carried
            att_ref[h] = att
            squares = squares + att * att
            crosses = crosses + go_ref[h].astype(F32) * att
        sums_ref[0] = squares
        sums_ref[1] = crosses
        return 0

    lax.fori_loop(0, owned, attend, 0)
    square = jnp.sum(sums_ref[0], axis=1, keepdims=True)
    cross = jnp.sum(sums_ref[1], axis=1, keepdims=True)
    first_half = lax.broadcasted_iota(jnp.int32, (tokens, width), 1) < width // 2
    stat_ref[...] = jnp.where(first_half, square, cross)

    def stat_copy(d, slot):
        return remote(
            stat_ref, other_ref.at[slot], stat_send.at[d - 1], stat_recv.at[slot], {"head": lax.rem(hd + d, nhead)}
        )

    for d in range(1, nhead):
        stat_copy(d, d - 1).start()
    for d in range(1, nhead):
        stat_copy(d, d - 1).wait()
    summed = stat_ref[...]
    for d in range(1, nhead):
        summed = summed + other_ref[d - 1]
    square = summed[:, 0:1]
    cross = summed[:, width // 2 : width // 2 + 1]
    mean_square = square / features + EPSILON
    inverse = lax.rsqrt(mean_square)
    norm_ref[...] = jnp.broadcast_to(inverse, (tokens, width))
    corr_ref[...] = jnp.broadcast_to(cross / (features * mean_square), (tokens, width))

    def back_local(i, _):
        for d in (1, 2, 3, 0):
            position = other(d)
            h = position * owned + i
            att = att_ref[h]
            normed_ref[h] = (att * norm_ref[...]).astype(BF16)
            grad = ((go_ref[h].astype(F32) - att * corr_ref[...]) * norm_ref[...]).astype(BF16)
            gattn_ref[h] = grad
            weight = jnp.where(epc_ref[...] == first_id, grow_ref[h], 0.0)
            decayed = (q_ref[h].astype(F32) * weight).astype(BF16)
            value = product(decayed, grad, 0, 0)
            below_rows = jnp.where(row == 0, pass_ref[pl.ds(h, 1), :], id_rows)
            if d == 0:
                bgroup_ref[c, i, 0:width] = value
                bgroup_ref[c, i, width:] = below_rows
            else:
                blocal_ref[h, 0:width] = value
                blocal_ref[h, width:] = below_rows
                up_copy(blocal_ref, bgroup_ref, bup_send, bup_recv, position, i).start()
        return 0

    lax.fori_loop(0, owned, back_local, 0)
    normed_store = pltpu.make_async_copy(normed_ref, normed_out, out_sem.at[0])
    normed_store.start()

    def backward_part(i):
        for position in range(GROUP):
            h = position * owned + i
            grad = gattn_ref[h]
            grad_score = (product(grad, v_ref[h], 1, 1) * decay_ref[h]).astype(BF16)
            carried = jnp.where(epc_ref[...] == prev_id, grow_ref[h], 0.0)
            low = state_ref[h].astype(BF16)
            gq_ref[h] = (
                product(grad_score, k_ref[h], 1, 0) + product(grad, low, 1, 1) * carried
            ).astype(BF16)
            kin_ref[h] = product(grad_score, q_ref[h], 0, 0)
            vin_ref[h] = product(score_ref[h], grad, 0, 0)

    scan(-1, backward_set, backward_part)
    gq_store = pltpu.make_async_copy(gq_ref, gq_out, out_sem.at[1])
    gq_store.start()

    def stores(h):
        return (
            pltpu.make_async_copy(gk_ref.at[h], gk_out.at[h], gk_sem.at[h]),
            pltpu.make_async_copy(gv_ref.at[h], gv_out.at[h], gv_sem.at[h]),
        )

    def finish(i, _):
        state_arrival(i, backward_set)
        for position in range(GROUP):
            h = position * owned + i
            trailing = jnp.where(epc_ref[...] == next_id, fall_ref[h], 0.0)
            low = bstate_ref[h].astype(BF16)
            gk_ref[h] = (kin_ref[h] + product(v_ref[h], low, 1, 1) * trailing).astype(BF16)
            gv_ref[h] = (vin_ref[h] + product(k_ref[h], low, 1, 0) * trailing).astype(BF16)
            for store in stores(h):
                store.start()
        return 0

    lax.fori_loop(0, owned, finish, 0)

    def settle_all(i, _):
        settle(i, 1, forward_set)
        settle(i, -1, backward_set)
        for position in range(GROUP):
            for store in stores(position * owned + i):
                store.wait()
        return 0

    lax.fori_loop(0, owned, settle_all, 0)
    normed_store.wait()
    gq_store.wait()


def hand_over(*refs):
    sources, targets, held, in_sem, out_sem = refs[:4], refs[4:8], refs[8], refs[9], refs[10]
    pairs = []
    for n in range(len(sources)):
        heads = sources[n].shape[0]
        for part in range(2):
            rows = pl.ds(part * heads // 2, heads // 2)
            slot = held.at[n, rows]
            pairs.append((
                pltpu.make_async_copy(sources[n].at[rows], slot, in_sem.at[n, part]),
                pltpu.make_async_copy(slot, targets[n].at[rows], out_sem.at[n, part]),
            ))
    for load, _ in pairs:
        load.start()
    for load, store in pairs:
        load.wait()
        store.start()
    for _, store in pairs:
        store.wait()


def per_device(nseq, nhead, query_rows, key_rows, value_rows, log_gate, episode, grad_out):
    heads, tokens, width = query_rows.shape
    owned = heads // GROUP
    padded = -(-heads // 8) * 8
    if padded != heads:
        log_gate = jnp.pad(log_gate, ((0, padded - heads), (0, 0)))
    reach = -(-min(REACH_MAX, nseq // 2) // GROUP)
    vmem = pl.BlockSpec(memory_space=pltpu.VMEM)
    outside = pl.BlockSpec(memory_space=pl.ANY)
    rows = jax.ShapeDtypeStruct(query_rows.shape, BF16)
    block = (heads, tokens, width)
    state_set = [
        pltpu.VMEM((heads, width + 8, width), F32),
        pltpu.VMEM((GROUP, owned, width + 8, width), F32),
        pltpu.VMEM((reach, owned, width + 8, width), F32),
        pltpu.VMEM((GROUP, owned, width, width), F32),
        pltpu.VMEM((owned, width + 8, width), F32),
        pltpu.VMEM((heads, width, width), F32),
    ]
    sem_set = [
        pltpu.SemaphoreType.DMA((GROUP, owned)),
        pltpu.SemaphoreType.DMA((GROUP, owned)),
        pltpu.SemaphoreType.DMA((reach, owned)),
        pltpu.SemaphoreType.DMA((reach, owned)),
        pltpu.SemaphoreType.DMA((GROUP, owned)),
        pltpu.SemaphoreType.DMA((GROUP, owned)),
    ]
    others = max(nhead - 1, 1)
    results = pl.pallas_call(
        functools.partial(kernel, nseq, nhead, float(heads * nhead * width)),
        out_shape=[rows] * 4,
        in_specs=[outside, outside, outside, vmem, vmem, outside],
        out_specs=[outside] * 4,
        scratch_shapes=[
            *[pltpu.VMEM(block, BF16)] * 8,
            pltpu.VMEM((padded, tokens), F32),
            pltpu.VMEM(block, F32),
            pltpu.VMEM(block, F32),
            pltpu.VMEM(block, F32),
            pltpu.VMEM((padded, width), F32),
            pltpu.VMEM((tokens, tokens), F32),
            pltpu.VMEM((tokens, width), F32),
            pltpu.VMEM((heads, tokens, tokens), F32),
            pltpu.VMEM((heads, tokens, tokens), BF16),
            pltpu.VMEM(block, F32),
            pltpu.VMEM(block, BF16),
            pltpu.VMEM(block, F32),
            pltpu.VMEM(block, F32),
            pltpu.VMEM((2, tokens, width), F32),
            pltpu.VMEM((tokens, width), F32),
            pltpu.VMEM((others, tokens, width), F32),
            pltpu.VMEM((tokens, width), F32),
            pltpu.VMEM((tokens, width), F32),
            pltpu.VMEM((8, width), F32),
            pltpu.VMEM((8, width), F32),
            pltpu.VMEM((8, width), F32),
            *state_set,
            *state_set,
            pltpu.SemaphoreType.DMA((4,)),
            pltpu.SemaphoreType.DMA((2,)),
            pltpu.SemaphoreType.DMA((heads,)),
            pltpu.SemaphoreType.DMA((heads,)),
            pltpu.SemaphoreType.DMA((2,)),
            pltpu.SemaphoreType.DMA((2,)),
            pltpu.SemaphoreType.DMA((others,)),
            pltpu.SemaphoreType.DMA((others,)),
            *sem_set,
            *sem_set,
        ],
        compiler_params=pltpu.CompilerParams(
            collective_id=0, has_side_effects=True, vmem_limit_bytes=56 * MIB
        ),
        cost_estimate=pl.CostEstimate(
            flops=heads * tokens * tokens * width * 18, bytes_accessed=heads * tokens * width * 16,
            transcendentals=heads * tokens * tokens,
        ),
    )(query_rows, key_rows, value_rows, log_gate, episode.reshape(1, tokens), grad_out)
    return pl.pallas_call(
        hand_over,
        out_shape=[rows] * 4,
        in_specs=[outside] * 4,
        out_specs=[outside] * 4,
        scratch_shapes=[
            pltpu.VMEM((4, *block), BF16),
            pltpu.SemaphoreType.DMA((4, 2)),
            pltpu.SemaphoreType.DMA((4, 2)),
        ],
        compiler_params=pltpu.CompilerParams(vmem_limit_bytes=56 * MIB),
    )(*results)


def solution(mesh):
    rows = P("head", "seq", None)
    return jax.shard_map(
        functools.partial(per_device, mesh.shape["seq"], mesh.shape["head"]),
        mesh=mesh,
        in_specs=(rows, rows, rows, P("head", "seq"), P("seq"), rows),
        out_specs=(rows, rows, rows, rows),
        check_vma=False,
    )
```

```python
import functools

import jax
import jax.numpy as jnp
from jax import lax
from jax.experimental import pallas as pl
from jax.experimental.pallas import tpu as pltpu
from jax.sharding import PartitionSpec as P

EPSILON = 1e-06
GROUP = 4
BLOCKED = -1e30
MIB = 1 << 20
F32 = jnp.float32
BF16 = jnp.bfloat16
MESH = pl.DeviceIdType.MESH


def product(a, b, over_a, over_b):
    return lax.dot_general(a, b, (((over_a,), (over_b,)), ((), ())), preferred_element_type=F32)


def kernel(
    nseq, nhead, features,
    q_in, k_in, v_in, gate_ref, ep_ref, go_in,
    normed_out, gq_out, gk_out, gv_out,
    q_ref, k_ref, v_ref, go_ref, normed_ref, gq_ref, gk_ref, gv_ref,
    run_ref, runc_ref, grow_ref, fall_ref, pass_ref, allow_ref, epc_ref, decay_ref, score_ref,
    att_ref, gattn_ref, kin_ref, vin_ref, sums_ref, stat_ref, other_ref, norm_ref, corr_ref,
    ids_ref, prev_ref, next_ref,
    local_ref, group_ref, chain_ref, leave_ref, enter_ref, state_ref,
    blocal_ref, bgroup_ref, bchain_ref, bleave_ref, benter_ref, bstate_ref,
    in_sem, out_sem, gk_sem, gv_sem, id_send, id_recv, stat_send, stat_recv,
    up_send, up_recv, chain_send, chain_recv, down_send, down_recv,
    bup_send, bup_recv, bchain_send, bchain_recv, bdown_send, bdown_recv,
):
    heads, tokens, width = q_ref.shape
    owned = heads // GROUP
    groups = nseq // GROUP
    reach = 2
    s = lax.axis_index("seq")
    hd = lax.axis_index("head")
    c = lax.rem(s, GROUP)
    z = s // GROUP
    base = s - c

    def member(position):
        return {"seq": base + position}

    def other(distance):
        return lax.rem(c + distance, GROUP)

    loads = [
        pltpu.make_async_copy(src, dst, in_sem.at[n])
        for n, (src, dst) in enumerate(((k_in, k_ref), (v_in, v_ref), (q_in, q_ref), (go_in, go_ref)))
    ]
    for load in loads:
        load.start()

    barrier = pltpu.get_barrier_semaphore()

    def greet(device):
        pl.semaphore_signal(barrier, inc=1, device_id=device, device_id_type=MESH)

    for d in range(1, GROUP):
        greet(member(other(d)))
    for d in range(1, nhead):
        greet({"head": lax.rem(hd + d, nhead)})

    @pl.when(s > 0)
    def _():
        greet({"seq": s - 1})

    @pl.when(s < nseq - 1)
    def _():
        greet({"seq": s + 1})

    for d in range(1, reach + 1):

        @pl.when(z >= d)
        def _():
            greet({"seq": s - GROUP * d})

        @pl.when(z < groups - d)
        def _():
            greet({"seq": s + GROUP * d})

    lane = lax.broadcasted_iota(jnp.int32, gate_ref.shape, 1)
    run = gate_ref[...]
    step = 1
    while step < tokens:
        run = run + jnp.where(lane >= step, pltpu.roll(run, step, 1), 0.0)
        step *= 2
    run_ref[...] = run
    total = run[:, tokens - 1 : tokens]
    fallen = jnp.exp(total - run).T
    for h in range(heads):
        fall_ref[h] = jnp.broadcast_to(fallen[:, h : h + 1], (tokens, width))
    pass_ref[...] = jnp.broadcast_to(jnp.exp(total), (total.shape[0], width))
    ep_row = ep_ref[...].astype(F32)
    ep_col = jnp.broadcast_to(jnp.broadcast_to(ep_row, (8, tokens)).T[:, 0:1], (tokens, width))
    epc_ref[...] = ep_col
    first_id = ep_row[:, 0:1]
    last_id = ep_row[:, tokens - 1 : tokens]
    half = lax.broadcasted_iota(jnp.int32, (8, width), 1) < width // 2
    ids_ref[...] = jnp.where(half, first_id, last_id)
    row = lax.broadcasted_iota(jnp.int32, (8, width), 0)
    id_rows = jnp.where(row == 1, last_id, first_id)
    loads[0].wait()
    loads[1].wait()

    def local_state(i, position, target, at):
        h = position * owned + i
        weight = jnp.where(epc_ref[...] == last_id, fall_ref[h], 0.0)
        decayed = (k_ref[h].astype(F32) * weight).astype(BF16)
        target[*at, 0:width] = product(decayed, v_ref[h], 0, 0)
        target[*at, width:] = jnp.where(row == 0, pass_ref[pl.ds(h, 1), :], id_rows)

    def local_states(i):
        for d in (1, 2, 3):
            local_state(i, other(d), local_ref, (other(d) * owned + i,))
        local_state(i, c, group_ref, (c, i))

    local_states(0)

    beside = jnp.minimum(s, 1) + jnp.minimum(nseq - 1 - s, 1)
    across = jnp.minimum(z, reach) + jnp.minimum(groups - 1 - z, reach)
    pl.semaphore_wait(barrier, GROUP - 1 + nhead - 1 + beside + across)

    def remote(src, dst, send, recv, device):
        return pltpu.make_async_remote_copy(
            src_ref=src, dst_ref=dst, send_sem=send, recv_sem=recv, device_id=device, device_id_type=MESH
        )

    def ids_after():
        return remote(ids_ref, prev_ref, id_send.at[0], id_recv.at[0], {"seq": s + 1})

    def ids_before():
        return remote(ids_ref, next_ref, id_send.at[1], id_recv.at[1], {"seq": s - 1})

    def up_copy(local, group, send, recv, position, i):
        return remote(
            local.at[position * owned + i], group.at[c, i], send.at[position, i], recv.at[c, i], member(position)
        )

    def up_arrival(local, group, send, recv, position, i):
        return remote(
            local.at[position * owned + i], group.at[position, i], send.at[position, i], recv.at[position, i],
            member(position),
        )

    def down_copy(leave, state, send, recv, position, i):
        return remote(
            leave.at[position, i], state.at[c * owned + i], send.at[position, i], recv.at[c, i], member(position)
        )

    def down_arrival(leave, state, send, recv, position, i):
        return remote(
            leave.at[position, i], state.at[position * owned + i], send.at[position, i], recv.at[position, i],
            member(position),
        )

    forward_set = (
        local_ref, group_ref, chain_ref, leave_ref, enter_ref, state_ref,
        up_send, up_recv, chain_send, chain_recv, down_send, down_recv,
    )
    backward_set = (
        blocal_ref, bgroup_ref, bchain_ref, bleave_ref, benter_ref, bstate_ref,
        bup_send, bup_recv, bchain_send, bchain_recv, bdown_send, bdown_recv,
    )

    def send_local(i, buffers):
        local, group, _, _, _, _, usend, urecv = buffers[:8]
        for d in (1, 2, 3):
            up_copy(local, group, usend, urecv, other(d), i).start()

    send_local(0, forward_set)

    @pl.when(s < nseq - 1)
    def _():
        ids_after().start()

    @pl.when(s > 0)
    def _():
        ids_before().start()

    def more_states(i, _):
        local_states(i)
        send_local(i, forward_set)
        return 0

    lax.fori_loop(1, owned, more_states, 0)

    columns = run.T
    grown = jnp.exp(run).T
    for h in range(heads):
        runc_ref[h] = jnp.broadcast_to(columns[:, h : h + 1], (tokens, width))
        grow_ref[h] = jnp.broadcast_to(grown[:, h : h + 1], (tokens, width))
    wide = jnp.concatenate([epc_ref[...]] * (tokens // width), axis=1)
    below = lax.broadcasted_iota(jnp.int32, (tokens, tokens), 0) >= lax.broadcasted_iota(
        jnp.int32, (tokens, tokens), 1
    )
    allow_ref[...] = jnp.where(below & (wide == ep_row), 0.0, BLOCKED)

    def chain_copy(buffers, i, slot, distance, sign):
        _, _, chain, _, enter, _, _, _, csend, crecv, _, _ = buffers
        return remote(
            enter.at[i], chain.at[slot, i], csend.at[distance - 1, i], crecv.at[slot, i],
            {"seq": s + sign * GROUP * distance},
        )

    def place(sign):
        return z if sign > 0 else groups - 1 - z

    def latter(sign):
        return lax.rem(place(sign), 2) == 1

    def send_total(i, sign, buffers):
        local, group, chain, leave, enter, state, usend, urecv, csend, crecv, dsend, drecv = buffers
        id_row = width + 1 if sign > 0 else width + 2
        for d in range(1, GROUP):
            up_arrival(local, group, usend, urecv, other(d), i).wait_recv()
        total_state = None
        for j in range(GROUP)[::sign]:
            factor = group[j, i, width : width + 1, :]
            mark = group[j, i, id_row : id_row + 1, :]
            if total_state is None:
                total_state = group[j, i, 0:width]
                factors = factor
            else:
                total_state = total_state * jnp.where(mark == before, factor, 0.0) + group[j, i, 0:width]
                factors = factors * factor
            before = mark
        enter[i, 0:width] = total_state
        enter[i, width:] = jnp.where(row == 0, factors, before)

        @pl.when(jnp.logical_not(latter(sign)))
        def _():
            chain_copy(buffers, i, 1, 1, sign).start()

    def send_entering(i, sign, buffers):
        local, group, chain, leave, enter, state, usend, urecv, csend, crecv, dsend, drecv = buffers
        id_row = width + 1 if sign > 0 else width + 2

        @pl.when(place(sign) < 2)
        def _():
            chain[0, i] = jnp.zeros((width + 8, width), F32)

        @pl.when(place(sign) >= 2)
        def _():
            chain_copy(buffers, i, 0, 1, -sign).wait_recv()

        @pl.when(latter(sign))
        def _():
            chain_copy(buffers, i, 1, 1, -sign).wait_recv()
            mark = chain[1, i, width + 1 : width + 2, :]
            factor = jnp.where(mark == chain[0, i, width + 1 : width + 2, :], chain[1, i, width : width + 1, :], 0.0)
            entering = chain[0, i, 0:width] * factor + chain[1, i, 0:width]
            chain[0, i, 0:width] = entering
            chain[0, i, width:] = jnp.broadcast_to(mark, (8, width))
            own = enter[i, width + 1 : width + 2, :]
            factor = jnp.where(own == mark, enter[i, width : width + 1, :], 0.0)
            enter[i, 0:width] = entering * factor + enter[i, 0:width]

            @pl.when(place(sign) < groups - 1)
            def _():
                chain_copy(buffers, i, 0, 1, sign).start()
                chain_copy(buffers, i, 0, 2, sign).start()

        carried = chain[0, i, 0:width]
        before = chain[0, i, width + 1 : width + 2, :]
        for n, j in enumerate(range(GROUP)[::sign]):
            leave[j, i] = carried
            if n < GROUP - 1:
                mark = group[j, i, id_row : id_row + 1, :]
                factor = jnp.where(mark == before, group[j, i, width : width + 1, :], 0.0)
                carried = carried * factor + group[j, i, 0:width]
                before = mark
        for d in range(1, GROUP):
            down_copy(leave, state, dsend, drecv, other(d), i).start()
        state[c * owned + i] = leave[c, i]

    def state_arrival(i, buffers):
        _, _, _, leave, _, state, _, _, _, _, dsend, drecv = buffers
        for d in range(1, GROUP):
            down_arrival(leave, state, dsend, drecv, other(d), i).wait_recv()

    def settle(i, sign, buffers):
        local, group, _, leave, _, state, usend, urecv, _, _, dsend, drecv = buffers
        for d in range(1, GROUP):
            up_arrival(local, group, usend, urecv, other(d), i).wait_send()
            down_arrival(leave, state, dsend, drecv, other(d), i).wait_send()

        @pl.when(place(sign) < groups - 1)
        def _():
            chain_copy(buffers, i, 0, 1, sign).wait_send()

        @pl.when(latter(sign) & (place(sign) < groups - 1))
        def _():
            chain_copy(buffers, i, 0, 2, sign).wait_send()

    def scan(sign, buffers, part):
        part(0)

        def steps(i, _):
            send_total(i, sign, buffers)

            @pl.when(i < owned - 1)
            def _():
                part(i + 1)

            send_entering(i, sign, buffers)
            return 0

        lax.fori_loop(0, owned, steps, 0)

    def forward_part(i):
        for position in range(GROUP):
            h = position * owned + i
            runc = jnp.concatenate([runc_ref[h]] * (tokens // width), axis=1)
            decay = jnp.exp(runc - run_ref[pl.ds(h, 1), :] + allow_ref[...])
            decay_ref[h] = decay
            score = (product(q_ref[h], k_ref[h], 1, 1) * decay).astype(BF16)
            score_ref[h] = score
            att_ref[h] = product(score, v_ref[h], 1, 0)

    loads[2].wait()
    scan(1, forward_set, forward_part)

    @pl.when(s == 0)
    def _():
        prev_ref[...] = jnp.full_like(prev_ref, -1.0)

    @pl.when(s == nseq - 1)
    def _():
        next_ref[...] = jnp.full_like(next_ref, -1.0)

    @pl.when(s < nseq - 1)
    def _():
        ids_after().wait_send()
        ids_before().wait_recv()

    @pl.when(s > 0)
    def _():
        ids_before().wait_send()
        ids_after().wait_recv()

    prev_id = prev_ref[0:1, width - 1 : width]
    next_id = next_ref[0:1, 0:1]
    loads[3].wait()

    sums_ref[...] = jnp.zeros_like(sums_ref)

    def attend(i, _):
        state_arrival(i, forward_set)
        squares = sums_ref[0]
        crosses = sums_ref[1]
        for position in range(GROUP):
            h = position * owned + i
            carried = jnp.where(epc_ref[...] == prev_id, grow_ref[h], 0.0)
            low = state_ref[h].astype(BF16)
            att = att_ref[h] + product(q_ref[h], low, 1, 0) * carried
            att_ref[h] = att
            squares = squares + att * att
            crosses = crosses + go_ref[h].astype(F32) * att
        sums_ref[0] = squares
        sums_ref[1] = crosses
        return 0

    lax.fori_loop(0, owned, attend, 0)
    square = jnp.sum(sums_ref[0], axis=1, keepdims=True)
    cross = jnp.sum(sums_ref[1], axis=1, keepdims=True)
    first_half = lax.broadcasted_iota(jnp.int32, (tokens, width), 1) < width // 2
    stat_ref[...] = jnp.where(first_half, square, cross)

    def stat_copy(d, slot):
        return remote(
            stat_ref, other_ref.at[slot], stat_send.at[d - 1], stat_recv.at[slot], {"head": lax.rem(hd + d, nhead)}
        )

    for d in range(1, nhead):
        stat_copy(d, d - 1).start()
    for d in range(1, nhead):
        stat_copy(d, d - 1).wait()
    summed = stat_ref[...]
    for d in range(1, nhead):
        summed = summed + other_ref[d - 1]
    square = summed[:, 0:1]
    cross = summed[:, width // 2 : width // 2 + 1]
    mean_square = square / features + EPSILON
    inverse = lax.rsqrt(mean_square)
    norm_ref[...] = jnp.broadcast_to(inverse, (tokens, width))
    corr_ref[...] = jnp.broadcast_to(cross / (features * mean_square), (tokens, width))

    def back_local(i, _):
        for d in (1, 2, 3, 0):
            position = other(d)
            h = position * owned + i
            att = att_ref[h]
            normed_ref[h] = (att * norm_ref[...]).astype(BF16)
            grad = ((go_ref[h].astype(F32) - att * corr_ref[...]) * norm_ref[...]).astype(BF16)
            gattn_ref[h] = grad
            weight = jnp.where(epc_ref[...] == first_id, grow_ref[h], 0.0)
            decayed = (q_ref[h].astype(F32) * weight).astype(BF16)
            value = product(decayed, grad, 0, 0)
            below_rows = jnp.where(row == 0, pass_ref[pl.ds(h, 1), :], id_rows)
            if d == 0:
                bgroup_ref[c, i, 0:width] = value
                bgroup_ref[c, i, width:] = below_rows
            else:
                blocal_ref[h, 0:width] = value
                blocal_ref[h, width:] = below_rows
                up_copy(blocal_ref, bgroup_ref, bup_send, bup_recv, position, i).start()
        return 0

    lax.fori_loop(0, owned, back_local, 0)
    normed_store = pltpu.make_async_copy(normed_ref, normed_out, out_sem.at[0])
    normed_store.start()

    def backward_part(i):
        for position in range(GROUP):
            h = position * owned + i
            grad = gattn_ref[h]
            grad_score = (product(grad, v_ref[h], 1, 1) * decay_ref[h]).astype(BF16)
            carried = jnp.where(epc_ref[...] == prev_id, grow_ref[h], 0.0)
            low = state_ref[h].astype(BF16)
            gq_ref[h] = (
                product(grad_score, k_ref[h], 1, 0) + product(grad, low, 1, 1) * carried
            ).astype(BF16)
            kin_ref[h] = product(grad_score, q_ref[h], 0, 0)
            vin_ref[h] = product(score_ref[h], grad, 0, 0)

    scan(-1, backward_set, backward_part)
    gq_store = pltpu.make_async_copy(gq_ref, gq_out, out_sem.at[1])
    gq_store.start()

    def stores(h):
        return (
            pltpu.make_async_copy(gk_ref.at[h], gk_out.at[h], gk_sem.at[h]),
            pltpu.make_async_copy(gv_ref.at[h], gv_out.at[h], gv_sem.at[h]),
        )

    def finish(i, _):
        state_arrival(i, backward_set)
        for position in range(GROUP):
            h = position * owned + i
            trailing = jnp.where(epc_ref[...] == next_id, fall_ref[h], 0.0)
            low = bstate_ref[h].astype(BF16)
            gk_ref[h] = (kin_ref[h] + product(v_ref[h], low, 1, 1) * trailing).astype(BF16)
            gv_ref[h] = (vin_ref[h] + product(k_ref[h], low, 1, 0) * trailing).astype(BF16)
            for store in stores(h):
                store.start()
        return 0

    lax.fori_loop(0, owned, finish, 0)

    def settle_all(i, _):
        settle(i, 1, forward_set)
        settle(i, -1, backward_set)
        for position in range(GROUP):
            for store in stores(position * owned + i):
                store.wait()
        return 0

    lax.fori_loop(0, owned, settle_all, 0)
    normed_store.wait()
    gq_store.wait()


def hand_over(*refs):
    sources, targets, held, in_sem, out_sem = refs[:4], refs[4:8], refs[8], refs[9], refs[10]
    pairs = []
    for n in range(len(sources)):
        heads = sources[n].shape[0]
        for part in range(2):
            rows = pl.ds(part * heads // 2, heads // 2)
            slot = held.at[n, rows]
            pairs.append((
                pltpu.make_async_copy(sources[n].at[rows], slot, in_sem.at[n, part]),
                pltpu.make_async_copy(slot, targets[n].at[rows], out_sem.at[n, part]),
            ))
    for load, _ in pairs:
        load.start()
    for load, store in pairs:
        load.wait()
        store.start()
    for _, store in pairs:
        store.wait()


def per_device(nseq, nhead, query_rows, key_rows, value_rows, log_gate, episode, grad_out):
    heads, tokens, width = query_rows.shape
    owned = heads // GROUP
    padded = -(-heads // 8) * 8
    if padded != heads:
        log_gate = jnp.pad(log_gate, ((0, padded - heads), (0, 0)))
    vmem = pl.BlockSpec(memory_space=pltpu.VMEM)
    outside = pl.BlockSpec(memory_space=pl.ANY)
    rows = jax.ShapeDtypeStruct(query_rows.shape, BF16)
    block = (heads, tokens, width)
    state_set = [
        pltpu.VMEM((heads, width + 8, width), F32),
        pltpu.VMEM((GROUP, owned, width + 8, width), F32),
        pltpu.VMEM((2, owned, width + 8, width), F32),
        pltpu.VMEM((GROUP, owned, width, width), F32),
        pltpu.VMEM((owned, width + 8, width), F32),
        pltpu.VMEM((heads, width, width), F32),
    ]
    sem_set = [
        pltpu.SemaphoreType.DMA((GROUP, owned)),
        pltpu.SemaphoreType.DMA((GROUP, owned)),
        pltpu.SemaphoreType.DMA((2, owned)),
        pltpu.SemaphoreType.DMA((2, owned)),
        pltpu.SemaphoreType.DMA((GROUP, owned)),
        pltpu.SemaphoreType.DMA((GROUP, owned)),
    ]
    others = max(nhead - 1, 1)
    results = pl.pallas_call(
        functools.partial(kernel, nseq, nhead, float(heads * nhead * width)),
        out_shape=[rows] * 4,
        in_specs=[outside, outside, outside, vmem, vmem, outside],
        out_specs=[outside] * 4,
        scratch_shapes=[
            *[pltpu.VMEM(block, BF16)] * 8,
            pltpu.VMEM((padded, tokens), F32),
            pltpu.VMEM(block, F32),
            pltpu.VMEM(block, F32),
            pltpu.VMEM(block, F32),
            pltpu.VMEM((padded, width), F32),
            pltpu.VMEM((tokens, tokens), F32),
            pltpu.VMEM((tokens, width), F32),
            pltpu.VMEM((heads, tokens, tokens), F32),
            pltpu.VMEM((heads, tokens, tokens), BF16),
            pltpu.VMEM(block, F32),
            pltpu.VMEM(block, BF16),
            pltpu.VMEM(block, F32),
            pltpu.VMEM(block, F32),
            pltpu.VMEM((2, tokens, width), F32),
            pltpu.VMEM((tokens, width), F32),
            pltpu.VMEM((others, tokens, width), F32),
            pltpu.VMEM((tokens, width), F32),
            pltpu.VMEM((tokens, width), F32),
            pltpu.VMEM((8, width), F32),
            pltpu.VMEM((8, width), F32),
            pltpu.VMEM((8, width), F32),
            *state_set,
            *state_set,
            pltpu.SemaphoreType.DMA((4,)),
            pltpu.SemaphoreType.DMA((2,)),
            pltpu.SemaphoreType.DMA((heads,)),
            pltpu.SemaphoreType.DMA((heads,)),
            pltpu.SemaphoreType.DMA((2,)),
            pltpu.SemaphoreType.DMA((2,)),
            pltpu.SemaphoreType.DMA((others,)),
            pltpu.SemaphoreType.DMA((others,)),
            *sem_set,
            *sem_set,
        ],
        compiler_params=pltpu.CompilerParams(
            collective_id=0, has_side_effects=True, vmem_limit_bytes=56 * MIB
        ),
        cost_estimate=pl.CostEstimate(
            flops=heads * tokens * tokens * width * 18, bytes_accessed=heads * tokens * width * 16,
            transcendentals=heads * tokens * tokens,
        ),
    )(query_rows, key_rows, value_rows, log_gate, episode.reshape(1, tokens), grad_out)
    return pl.pallas_call(
        hand_over,
        out_shape=[rows] * 4,
        in_specs=[outside] * 4,
        out_specs=[outside] * 4,
        scratch_shapes=[
            pltpu.VMEM((4, *block), BF16),
            pltpu.SemaphoreType.DMA((4, 2)),
            pltpu.SemaphoreType.DMA((4, 2)),
        ],
        compiler_params=pltpu.CompilerParams(vmem_limit_bytes=56 * MIB),
    )(*results)


def solution(mesh):
    rows = P("head", "seq", None)
    return jax.shard_map(
        functools.partial(per_device, mesh.shape["seq"], mesh.shape["head"]),
        mesh=mesh,
        in_specs=(rows, rows, rows, P("head", "seq"), P("seq"), rows),
        out_specs=(rows, rows, rows, rows),
        check_vma=False,
    )
```

```python
import functools

import jax
import jax.numpy as jnp
from jax import lax
from jax.experimental import pallas as pl
from jax.experimental.pallas import tpu as pltpu
from jax.sharding import PartitionSpec as P

EPSILON = 1e-06
GROUP = 4
BLOCKED = -1e30
MIB = 1 << 20
F32 = jnp.float32
BF16 = jnp.bfloat16
MESH = pl.DeviceIdType.MESH


def product(a, b, over_a, over_b):
    return lax.dot_general(a, b, (((over_a,), (over_b,)), ((), ())), preferred_element_type=F32)


def kernel(
    nseq, nhead, features,
    q_in, k_in, v_in, gate_ref, ep_ref, go_in,
    normed_out, gq_out, gk_out, gv_out,
    q_ref, k_ref, v_ref, go_ref, normed_ref, gq_ref, gk_ref, gv_ref,
    run_ref, runc_ref, grow_ref, fall_ref, pass_ref, allow_ref, epc_ref, decay_ref, score_ref,
    att_ref, gattn_ref, kin_ref, vin_ref, sums_ref, stat_ref, other_ref, norm_ref, corr_ref,
    ids_ref, prev_ref, next_ref,
    local_ref, group_ref, chain_ref, leave_ref, enter_ref, state_ref,
    blocal_ref, bgroup_ref, bchain_ref, bleave_ref, benter_ref, bstate_ref,
    in_sem, out_sem, gk_sem, gv_sem, id_send, id_recv, stat_send, stat_recv,
    up_send, up_recv, chain_send, chain_recv, down_send, down_recv,
    bup_send, bup_recv, bchain_send, bchain_recv, bdown_send, bdown_recv,
):
    heads, tokens, width = q_ref.shape
    owned = heads // GROUP
    groups = nseq // GROUP
    reach = 2
    s = lax.axis_index("seq")
    hd = lax.axis_index("head")
    c = lax.rem(s, GROUP)
    z = s // GROUP
    base = s - c

    def member(position):
        return {"seq": base + position}

    def other(distance):
        return lax.rem(c + distance, GROUP)

    loads = [
        pltpu.make_async_copy(src, dst, in_sem.at[n])
        for n, (src, dst) in enumerate(((k_in, k_ref), (v_in, v_ref), (q_in, q_ref), (go_in, go_ref)))
    ]
    for load in loads:
        load.start()

    barrier = pltpu.get_barrier_semaphore()

    def greet(device):
        pl.semaphore_signal(barrier, inc=1, device_id=device, device_id_type=MESH)

    for d in range(1, GROUP):
        greet(member(other(d)))
    for d in range(1, nhead):
        greet({"head": lax.rem(hd + d, nhead)})

    @pl.when(s > 0)
    def _():
        greet({"seq": s - 1})

    @pl.when(s < nseq - 1)
    def _():
        greet({"seq": s + 1})

    for d in range(1, reach + 1):

        @pl.when(z >= d)
        def _():
            greet({"seq": s - GROUP * d})

        @pl.when(z < groups - d)
        def _():
            greet({"seq": s + GROUP * d})

    lane = lax.broadcasted_iota(jnp.int32, gate_ref.shape, 1)
    run = gate_ref[...]
    step = 1
    while step < tokens:
        run = run + jnp.where(lane >= step, pltpu.roll(run, step, 1), 0.0)
        step *= 2
    run_ref[...] = run
    total = run[:, tokens - 1 : tokens]
    fallen = jnp.exp(total - run).T
    for h in range(heads):
        fall_ref[h] = jnp.broadcast_to(fallen[:, h : h + 1], (tokens, width))
    pass_ref[...] = jnp.broadcast_to(jnp.exp(total), (total.shape[0], width))
    ep_row = ep_ref[...].astype(F32)
    ep_col = jnp.broadcast_to(jnp.broadcast_to(ep_row, (8, tokens)).T[:, 0:1], (tokens, width))
    epc_ref[...] = ep_col
    first_id = ep_row[:, 0:1]
    last_id = ep_row[:, tokens - 1 : tokens]
    half = lax.broadcasted_iota(jnp.int32, (8, width), 1) < width // 2
    ids_ref[...] = jnp.where(half, first_id, last_id)
    row = lax.broadcasted_iota(jnp.int32, (8, width), 0)
    id_rows = jnp.where(row == 1, last_id, first_id)
    loads[0].wait()
    loads[1].wait()

    def local_state(i, position, target, at):
        h = position * owned + i
        weight = jnp.where(epc_ref[...] == last_id, fall_ref[h], 0.0)
        decayed = (k_ref[h].astype(F32) * weight).astype(BF16)
        target[*at, 0:width] = product(decayed, v_ref[h], 0, 0)
        target[*at, width:] = jnp.where(row == 0, pass_ref[pl.ds(h, 1), :], id_rows)

    def local_states(i):
        for d in (1, 2, 3):
            local_state(i, other(d), local_ref, (other(d) * owned + i,))
        local_state(i, c, group_ref, (c, i))

    local_states(0)

    beside = jnp.minimum(s, 1) + jnp.minimum(nseq - 1 - s, 1)
    across = jnp.minimum(z, reach) + jnp.minimum(groups - 1 - z, reach)
    pl.semaphore_wait(barrier, GROUP - 1 + nhead - 1 + beside + across)

    def remote(src, dst, send, recv, device):
        return pltpu.make_async_remote_copy(
            src_ref=src, dst_ref=dst, send_sem=send, recv_sem=recv, device_id=device, device_id_type=MESH
        )

    def ids_after():
        return remote(ids_ref, prev_ref, id_send.at[0], id_recv.at[0], {"seq": s + 1})

    def ids_before():
        return remote(ids_ref, next_ref, id_send.at[1], id_recv.at[1], {"seq": s - 1})

    def up_copy(local, group, send, recv, position, i):
        return remote(
            local.at[position * owned + i], group.at[c, i], send.at[position, i], recv.at[c, i], member(position)
        )

    def up_arrival(local, group, send, recv, position, i):
        return remote(
            local.at[position * owned + i], group.at[position, i], send.at[position, i], recv.at[position, i],
            member(position),
        )

    def down_copy(leave, state, send, recv, position, i):
        return remote(
            leave.at[position, i], state.at[c * owned + i], send.at[position, i], recv.at[c, i], member(position)
        )

    def down_arrival(leave, state, send, recv, position, i):
        return remote(
            leave.at[position, i], state.at[position * owned + i], send.at[position, i], recv.at[position, i],
            member(position),
        )

    forward_set = (
        local_ref, group_ref, chain_ref, leave_ref, enter_ref, state_ref,
        up_send, up_recv, chain_send, chain_recv, down_send, down_recv,
    )
    backward_set = (
        blocal_ref, bgroup_ref, bchain_ref, bleave_ref, benter_ref, bstate_ref,
        bup_send, bup_recv, bchain_send, bchain_recv, bdown_send, bdown_recv,
    )

    def send_local(i, buffers):
        local, group, _, _, _, _, usend, urecv = buffers[:8]
        for d in (1, 2, 3):
            up_copy(local, group, usend, urecv, other(d), i).start()

    send_local(0, forward_set)

    @pl.when(s < nseq - 1)
    def _():
        ids_after().start()

    @pl.when(s > 0)
    def _():
        ids_before().start()

    def more_states(i, _):
        local_states(i)
        send_local(i, forward_set)
        return 0

    lax.fori_loop(1, owned, more_states, 0)

    columns = run.T
    grown = jnp.exp(run).T
    for h in range(heads):
        runc_ref[h] = jnp.broadcast_to(columns[:, h : h + 1], (tokens, width))
        grow_ref[h] = jnp.broadcast_to(grown[:, h : h + 1], (tokens, width))
    wide = jnp.concatenate([epc_ref[...]] * (tokens // width), axis=1)
    below = lax.broadcasted_iota(jnp.int32, (tokens, tokens), 0) >= lax.broadcasted_iota(
        jnp.int32, (tokens, tokens), 1
    )
    allow_ref[...] = jnp.where(below & (wide == ep_row), 0.0, BLOCKED)

    def chain_copy(buffers, i, slot, distance, sign):
        _, _, chain, _, enter, _, _, _, csend, crecv, _, _ = buffers
        return remote(
            enter.at[i], chain.at[slot, i], csend.at[distance - 1, i], crecv.at[slot, i],
            {"seq": s + sign * GROUP * distance},
        )

    def place(sign):
        return z if sign > 0 else groups - 1 - z

    def latter(sign):
        return lax.rem(place(sign), 2) == 1

    def send_total(i, sign, buffers):
        local, group, chain, leave, enter, state, usend, urecv, csend, crecv, dsend, drecv = buffers
        id_row = width + 1 if sign > 0 else width + 2
        for d in range(1, GROUP):
            up_arrival(local, group, usend, urecv, other(d), i).wait_recv()
        total_state = None
        for j in range(GROUP)[::sign]:
            factor = group[j, i, width : width + 1, :]
            mark = group[j, i, id_row : id_row + 1, :]
            if total_state is None:
                total_state = group[j, i, 0:width]
                factors = factor
            else:
                total_state = total_state * jnp.where(mark == before, factor, 0.0) + group[j, i, 0:width]
                factors = factors * factor
            before = mark
        enter[i, 0:width] = total_state
        enter[i, width:] = jnp.where(row == 0, factors, before)

        @pl.when(jnp.logical_not(latter(sign)))
        def _():
            chain_copy(buffers, i, 1, 1, sign).start()

    def receive_state(i, sign, buffers):
        chain = buffers[2]

        @pl.when(place(sign) < 2)
        def _():
            chain[0, i] = jnp.zeros((width + 8, width), F32)

        @pl.when(place(sign) >= 2)
        def _():
            chain_copy(buffers, i, 0, 1, -sign).wait_recv()

    def join_pair(i, sign, buffers):
        chain, enter = buffers[2], buffers[4]
        receive_state(i, sign, buffers)
        chain_copy(buffers, i, 1, 1, -sign).wait_recv()
        mark = chain[1, i, width + 1 : width + 2, :]
        factor = jnp.where(mark == chain[0, i, width + 1 : width + 2, :], chain[1, i, width : width + 1, :], 0.0)
        entering = chain[0, i, 0:width] * factor + chain[1, i, 0:width]
        chain[0, i, 0:width] = entering
        chain[0, i, width:] = jnp.broadcast_to(mark, (8, width))
        own = enter[i, width + 1 : width + 2, :]
        factor = jnp.where(own == mark, enter[i, width : width + 1, :], 0.0)
        enter[i, 0:width] = entering * factor + enter[i, 0:width]

    def send_next(i, sign, buffers):
        @pl.when(latter(sign) & (place(sign) < groups - 1))
        def _():
            join_pair(i, sign, buffers)
            chain_copy(buffers, i, 0, 1, sign).start()
            chain_copy(buffers, i, 0, 2, sign).start()

    def send_entering(i, sign, buffers):
        local, group, chain, leave, enter, state, usend, urecv, csend, crecv, dsend, drecv = buffers
        id_row = width + 1 if sign > 0 else width + 2

        @pl.when(place(sign) == groups - 1)
        def _():
            join_pair(i, sign, buffers)

        @pl.when(jnp.logical_not(latter(sign)))
        def _():
            receive_state(i, sign, buffers)

        carried = chain[0, i, 0:width]
        before = chain[0, i, width + 1 : width + 2, :]
        for n, j in enumerate(range(GROUP)[::sign]):
            leave[j, i] = carried
            if n < GROUP - 1:
                mark = group[j, i, id_row : id_row + 1, :]
                factor = jnp.where(mark == before, group[j, i, width : width + 1, :], 0.0)
                carried = carried * factor + group[j, i, 0:width]
                before = mark
        for d in range(1, GROUP):
            down_copy(leave, state, dsend, drecv, other(d), i).start()
        state[c * owned + i] = leave[c, i]

    def state_arrival(i, buffers):
        _, _, _, leave, _, state, _, _, _, _, dsend, drecv = buffers
        for d in range(1, GROUP):
            down_arrival(leave, state, dsend, drecv, other(d), i).wait_recv()

    def settle(i, sign, buffers):
        local, group, _, leave, _, state, usend, urecv, _, _, dsend, drecv = buffers
        for d in range(1, GROUP):
            up_arrival(local, group, usend, urecv, other(d), i).wait_send()
            down_arrival(leave, state, dsend, drecv, other(d), i).wait_send()

        @pl.when(place(sign) < groups - 1)
        def _():
            chain_copy(buffers, i, 0, 1, sign).wait_send()

        @pl.when(latter(sign) & (place(sign) < groups - 1))
        def _():
            chain_copy(buffers, i, 0, 2, sign).wait_send()

    def scan(sign, buffers, part):
        def steps(i, _):
            send_total(i, sign, buffers)
            part(i)
            send_next(i, sign, buffers)

            @pl.when(i > 0)
            def _():
                send_entering(i - 1, sign, buffers)

            return 0

        lax.fori_loop(0, owned, steps, 0)
        send_entering(owned - 1, sign, buffers)

    def forward_part(i):
        for position in range(GROUP):
            h = position * owned + i
            runc = jnp.concatenate([runc_ref[h]] * (tokens // width), axis=1)
            decay = jnp.exp(runc - run_ref[pl.ds(h, 1), :] + allow_ref[...])
            decay_ref[h] = decay
            score = (product(q_ref[h], k_ref[h], 1, 1) * decay).astype(BF16)
            score_ref[h] = score
            att_ref[h] = product(score, v_ref[h], 1, 0)

    loads[2].wait()
    scan(1, forward_set, forward_part)

    @pl.when(s == 0)
    def _():
        prev_ref[...] = jnp.full_like(prev_ref, -1.0)

    @pl.when(s == nseq - 1)
    def _():
        next_ref[...] = jnp.full_like(next_ref, -1.0)

    @pl.when(s < nseq - 1)
    def _():
        ids_after().wait_send()
        ids_before().wait_recv()

    @pl.when(s > 0)
    def _():
        ids_before().wait_send()
        ids_after().wait_recv()

    prev_id = prev_ref[0:1, width - 1 : width]
    next_id = next_ref[0:1, 0:1]
    loads[3].wait()

    sums_ref[...] = jnp.zeros_like(sums_ref)

    def attend(i, _):
        state_arrival(i, forward_set)
        squares = sums_ref[0]
        crosses = sums_ref[1]
        for position in range(GROUP):
            h = position * owned + i
            carried = jnp.where(epc_ref[...] == prev_id, grow_ref[h], 0.0)
            low = state_ref[h].astype(BF16)
            att = att_ref[h] + product(q_ref[h], low, 1, 0) * carried
            att_ref[h] = att
            squares = squares + att * att
            crosses = crosses + go_ref[h].astype(F32) * att
        sums_ref[0] = squares
        sums_ref[1] = crosses
        return 0

    lax.fori_loop(0, owned, attend, 0)
    square = jnp.sum(sums_ref[0], axis=1, keepdims=True)
    cross = jnp.sum(sums_ref[1], axis=1, keepdims=True)
    first_half = lax.broadcasted_iota(jnp.int32, (tokens, width), 1) < width // 2
    stat_ref[...] = jnp.where(first_half, square, cross)

    def stat_copy(d, slot):
        return remote(
            stat_ref, other_ref.at[slot], stat_send.at[d - 1], stat_recv.at[slot], {"head": lax.rem(hd + d, nhead)}
        )

    for d in range(1, nhead):
        stat_copy(d, d - 1).start()
    for d in range(1, nhead):
        stat_copy(d, d - 1).wait()
    summed = stat_ref[...]
    for d in range(1, nhead):
        summed = summed + other_ref[d - 1]
    square = summed[:, 0:1]
    cross = summed[:, width // 2 : width // 2 + 1]
    mean_square = square / features + EPSILON
    inverse = lax.rsqrt(mean_square)
    norm_ref[...] = jnp.broadcast_to(inverse, (tokens, width))
    corr_ref[...] = jnp.broadcast_to(cross / (features * mean_square), (tokens, width))

    def back_local(i, _):
        for d in (1, 2, 3, 0):
            position = other(d)
            h = position * owned + i
            att = att_ref[h]
            normed_ref[h] = (att * norm_ref[...]).astype(BF16)
            grad = ((go_ref[h].astype(F32) - att * corr_ref[...]) * norm_ref[...]).astype(BF16)
            gattn_ref[h] = grad
            weight = jnp.where(epc_ref[...] == first_id, grow_ref[h], 0.0)
            decayed = (q_ref[h].astype(F32) * weight).astype(BF16)
            value = product(decayed, grad, 0, 0)
            below_rows = jnp.where(row == 0, pass_ref[pl.ds(h, 1), :], id_rows)
            if d == 0:
                bgroup_ref[c, i, 0:width] = value
                bgroup_ref[c, i, width:] = below_rows
            else:
                blocal_ref[h, 0:width] = value
                blocal_ref[h, width:] = below_rows
                up_copy(blocal_ref, bgroup_ref, bup_send, bup_recv, position, i).start()
        return 0

    lax.fori_loop(0, owned, back_local, 0)
    normed_store = pltpu.make_async_copy(normed_ref, normed_out, out_sem.at[0])
    normed_store.start()

    def backward_part(i):
        for position in range(GROUP):
            h = position * owned + i
            grad = gattn_ref[h]
            grad_score = (product(grad, v_ref[h], 1, 1) * decay_ref[h]).astype(BF16)
            carried = jnp.where(epc_ref[...] == prev_id, grow_ref[h], 0.0)
            low = state_ref[h].astype(BF16)
            gq_ref[h] = (
                product(grad_score, k_ref[h], 1, 0) + product(grad, low, 1, 1) * carried
            ).astype(BF16)
            kin_ref[h] = product(grad_score, q_ref[h], 0, 0)
            vin_ref[h] = product(score_ref[h], grad, 0, 0)

    scan(-1, backward_set, backward_part)
    gq_store = pltpu.make_async_copy(gq_ref, gq_out, out_sem.at[1])
    gq_store.start()

    def stores(h):
        return (
            pltpu.make_async_copy(gk_ref.at[h], gk_out.at[h], gk_sem.at[h]),
            pltpu.make_async_copy(gv_ref.at[h], gv_out.at[h], gv_sem.at[h]),
        )

    def finish(i, _):
        state_arrival(i, backward_set)
        for position in range(GROUP):
            h = position * owned + i
            trailing = jnp.where(epc_ref[...] == next_id, fall_ref[h], 0.0)
            low = bstate_ref[h].astype(BF16)
            gk_ref[h] = (kin_ref[h] + product(v_ref[h], low, 1, 1) * trailing).astype(BF16)
            gv_ref[h] = (vin_ref[h] + product(k_ref[h], low, 1, 0) * trailing).astype(BF16)
            for store in stores(h):
                store.start()
        return 0

    lax.fori_loop(0, owned, finish, 0)

    def settle_all(i, _):
        settle(i, 1, forward_set)
        settle(i, -1, backward_set)
        for position in range(GROUP):
            for store in stores(position * owned + i):
                store.wait()
        return 0

    lax.fori_loop(0, owned, settle_all, 0)
    normed_store.wait()
    gq_store.wait()


def hand_over(*refs):
    sources, targets, held, in_sem, out_sem = refs[:4], refs[4:8], refs[8], refs[9], refs[10]
    pairs = []
    for n in range(len(sources)):
        heads = sources[n].shape[0]
        for part in range(2):
            rows = pl.ds(part * heads // 2, heads // 2)
            slot = held.at[n, rows]
            pairs.append((
                pltpu.make_async_copy(sources[n].at[rows], slot, in_sem.at[n, part]),
                pltpu.make_async_copy(slot, targets[n].at[rows], out_sem.at[n, part]),
            ))
    for load, _ in pairs:
        load.start()
    for load, store in pairs:
        load.wait()
        store.start()
    for _, store in pairs:
        store.wait()


def per_device(nseq, nhead, query_rows, key_rows, value_rows, log_gate, episode, grad_out):
    heads, tokens, width = query_rows.shape
    owned = heads // GROUP
    padded = -(-heads // 8) * 8
    if padded != heads:
        log_gate = jnp.pad(log_gate, ((0, padded - heads), (0, 0)))
    vmem = pl.BlockSpec(memory_space=pltpu.VMEM)
    outside = pl.BlockSpec(memory_space=pl.ANY)
    rows = jax.ShapeDtypeStruct(query_rows.shape, BF16)
    block = (heads, tokens, width)
    state_set = [
        pltpu.VMEM((heads, width + 8, width), F32),
        pltpu.VMEM((GROUP, owned, width + 8, width), F32),
        pltpu.VMEM((2, owned, width + 8, width), F32),
        pltpu.VMEM((GROUP, owned, width, width), F32),
        pltpu.VMEM((owned, width + 8, width), F32),
        pltpu.VMEM((heads, width, width), F32),
    ]
    sem_set = [
        pltpu.SemaphoreType.DMA((GROUP, owned)),
        pltpu.SemaphoreType.DMA((GROUP, owned)),
        pltpu.SemaphoreType.DMA((2, owned)),
        pltpu.SemaphoreType.DMA((2, owned)),
        pltpu.SemaphoreType.DMA((GROUP, owned)),
        pltpu.SemaphoreType.DMA((GROUP, owned)),
    ]
    others = max(nhead - 1, 1)
    results = pl.pallas_call(
        functools.partial(kernel, nseq, nhead, float(heads * nhead * width)),
        out_shape=[rows] * 4,
        in_specs=[outside, outside, outside, vmem, vmem, outside],
        out_specs=[outside] * 4,
        scratch_shapes=[
            *[pltpu.VMEM(block, BF16)] * 8,
            pltpu.VMEM((padded, tokens), F32),
            pltpu.VMEM(block, F32),
            pltpu.VMEM(block, F32),
            pltpu.VMEM(block, F32),
            pltpu.VMEM((padded, width), F32),
            pltpu.VMEM((tokens, tokens), F32),
            pltpu.VMEM((tokens, width), F32),
            pltpu.VMEM((heads, tokens, tokens), F32),
            pltpu.VMEM((heads, tokens, tokens), BF16),
            pltpu.VMEM(block, F32),
            pltpu.VMEM(block, BF16),
            pltpu.VMEM(block, F32),
            pltpu.VMEM(block, F32),
            pltpu.VMEM((2, tokens, width), F32),
            pltpu.VMEM((tokens, width), F32),
            pltpu.VMEM((others, tokens, width), F32),
            pltpu.VMEM((tokens, width), F32),
            pltpu.VMEM((tokens, width), F32),
            pltpu.VMEM((8, width), F32),
            pltpu.VMEM((8, width), F32),
            pltpu.VMEM((8, width), F32),
            *state_set,
            *state_set,
            pltpu.SemaphoreType.DMA((4,)),
            pltpu.SemaphoreType.DMA((2,)),
            pltpu.SemaphoreType.DMA((heads,)),
            pltpu.SemaphoreType.DMA((heads,)),
            pltpu.SemaphoreType.DMA((2,)),
            pltpu.SemaphoreType.DMA((2,)),
            pltpu.SemaphoreType.DMA((others,)),
            pltpu.SemaphoreType.DMA((others,)),
            *sem_set,
            *sem_set,
        ],
        compiler_params=pltpu.CompilerParams(
            collective_id=0, has_side_effects=True, vmem_limit_bytes=56 * MIB
        ),
        cost_estimate=pl.CostEstimate(
            flops=heads * tokens * tokens * width * 18, bytes_accessed=heads * tokens * width * 16,
            transcendentals=heads * tokens * tokens,
        ),
    )(query_rows, key_rows, value_rows, log_gate, episode.reshape(1, tokens), grad_out)
    return pl.pallas_call(
        hand_over,
        out_shape=[rows] * 4,
        in_specs=[outside] * 4,
        out_specs=[outside] * 4,
        scratch_shapes=[
            pltpu.VMEM((4, *block), BF16),
            pltpu.SemaphoreType.DMA((4, 2)),
            pltpu.SemaphoreType.DMA((4, 2)),
        ],
        compiler_params=pltpu.CompilerParams(vmem_limit_bytes=56 * MIB),
    )(*results)


def solution(mesh):
    rows = P("head", "seq", None)
    return jax.shard_map(
        functools.partial(per_device, mesh.shape["seq"], mesh.shape["head"]),
        mesh=mesh,
        in_specs=(rows, rows, rows, P("head", "seq"), P("seq"), rows),
        out_specs=(rows, rows, rows, rows),
        check_vma=False,
    )
```

```python
import functools

import jax
import jax.numpy as jnp
from jax import lax
from jax.experimental import pallas as pl
from jax.experimental.pallas import tpu as pltpu
from jax.sharding import PartitionSpec as P

EPSILON = 1e-06
GROUP = 4
BLOCKED = -1e30
MIB = 1 << 20
F32 = jnp.float32
BF16 = jnp.bfloat16
MESH = pl.DeviceIdType.MESH


def product(a, b, over_a, over_b):
    return lax.dot_general(a, b, (((over_a,), (over_b,)), ((), ())), preferred_element_type=F32)


def kernel(
    nseq, nhead, features,
    q_in, k_in, v_in, gate_ref, ep_ref, go_in,
    normed_out, gq_out, gk_out, gv_out,
    q_ref, k_ref, v_ref, go_ref, normed_ref, gq_ref, gk_ref, gv_ref,
    run_ref, runc_ref, grow_ref, fall_ref, pass_ref, allow_ref, epc_ref, decay_ref, score_ref,
    att_ref, gattn_ref, kin_ref, vin_ref, sums_ref, stat_ref, other_ref, norm_ref, corr_ref,
    ids_ref, prev_ref, next_ref, marks_ref, group_marks_ref,
    local_ref, group_ref, chain_ref, leave_ref, enter_ref, state_ref,
    blocal_ref, bgroup_ref, bchain_ref, bleave_ref, benter_ref, bstate_ref,
    marks_send, marks_recv, in_sem, out_sem, gk_sem, gv_sem, id_send, id_recv, stat_send, stat_recv,
    up_send, up_recv, chain_send, chain_recv, down_send, down_recv,
    bup_send, bup_recv, bchain_send, bchain_recv, bdown_send, bdown_recv,
):
    heads, tokens, width = q_ref.shape
    owned = heads // GROUP
    groups = nseq // GROUP
    reach = 2
    s = lax.axis_index("seq")
    hd = lax.axis_index("head")
    c = lax.rem(s, GROUP)
    z = s // GROUP
    base = s - c

    def member(position):
        return {"seq": base + position}

    def other(distance):
        return lax.rem(c + distance, GROUP)

    loads = [
        pltpu.make_async_copy(src, dst, in_sem.at[n])
        for n, (src, dst) in enumerate(((k_in, k_ref), (v_in, v_ref), (q_in, q_ref), (go_in, go_ref)))
    ]
    for load in loads:
        load.start()

    barrier = pltpu.get_barrier_semaphore()

    def greet(device):
        pl.semaphore_signal(barrier, inc=1, device_id=device, device_id_type=MESH)

    for d in range(1, GROUP):
        greet(member(other(d)))
    for d in range(1, nhead):
        greet({"head": lax.rem(hd + d, nhead)})

    @pl.when(s > 0)
    def _():
        greet({"seq": s - 1})

    @pl.when(s < nseq - 1)
    def _():
        greet({"seq": s + 1})

    for d in range(1, reach + 1):

        @pl.when(z >= d)
        def _():
            greet({"seq": s - GROUP * d})

        @pl.when(z < groups - d)
        def _():
            greet({"seq": s + GROUP * d})

    lane = lax.broadcasted_iota(jnp.int32, gate_ref.shape, 1)
    run = gate_ref[...]
    step = 1
    while step < tokens:
        run = run + jnp.where(lane >= step, pltpu.roll(run, step, 1), 0.0)
        step *= 2
    run_ref[...] = run
    total = run[:, tokens - 1 : tokens]
    fallen = jnp.exp(total - run).T
    for h in range(heads):
        fall_ref[h] = jnp.broadcast_to(fallen[:, h : h + 1], (tokens, width))
    pass_ref[...] = jnp.broadcast_to(jnp.exp(total), (total.shape[0], width))
    ep_row = ep_ref[...].astype(F32)
    ep_col = jnp.broadcast_to(jnp.broadcast_to(ep_row, (8, tokens)).T[:, 0:1], (tokens, width))
    epc_ref[...] = ep_col
    first_id = ep_row[:, 0:1]
    last_id = ep_row[:, tokens - 1 : tokens]
    half = lax.broadcasted_iota(jnp.int32, (8, width), 1) < width // 2
    ids_ref[...] = jnp.where(half, first_id, last_id)
    row = lax.broadcasted_iota(jnp.int32, (8, width), 0)
    for position in range(GROUP):
        marks_ref[position] = jnp.where(row == owned, last_id, first_id)
        marks_ref[position, 0:owned] = pass_ref[position * owned : (position + 1) * owned, :]
    group_marks_ref[c] = marks_ref[c]
    loads[0].wait()
    loads[1].wait()

    def local_state(i, position, target, at):
        h = position * owned + i
        weight = jnp.where(epc_ref[...] == last_id, fall_ref[h], 0.0)
        decayed = (k_ref[h].astype(F32) * weight).astype(BF16)
        target[*at] = product(decayed, v_ref[h], 0, 0)

    def local_states(i):
        for d in (1, 2, 3):
            local_state(i, other(d), local_ref, (other(d) * owned + i,))
        local_state(i, c, group_ref, (c, i))

    local_states(0)

    beside = jnp.minimum(s, 1) + jnp.minimum(nseq - 1 - s, 1)
    across = jnp.minimum(z, reach) + jnp.minimum(groups - 1 - z, reach)
    pl.semaphore_wait(barrier, GROUP - 1 + nhead - 1 + beside + across)

    def remote(src, dst, send, recv, device):
        return pltpu.make_async_remote_copy(
            src_ref=src, dst_ref=dst, send_sem=send, recv_sem=recv, device_id=device, device_id_type=MESH
        )

    def ids_after():
        return remote(ids_ref, prev_ref, id_send.at[0], id_recv.at[0], {"seq": s + 1})

    def ids_before():
        return remote(ids_ref, next_ref, id_send.at[1], id_recv.at[1], {"seq": s - 1})

    def up_copy(local, group, send, recv, position, i):
        return remote(
            local.at[position * owned + i], group.at[c, i], send.at[position, i], recv.at[c, i], member(position)
        )

    def up_arrival(local, group, send, recv, position, i):
        return remote(
            local.at[position * owned + i], group.at[position, i], send.at[position, i], recv.at[position, i],
            member(position),
        )

    def down_copy(leave, state, send, recv, position, i):
        return remote(
            leave.at[position, i], state.at[c * owned + i], send.at[position, i], recv.at[c, i], member(position)
        )

    def down_arrival(leave, state, send, recv, position, i):
        return remote(
            leave.at[position, i], state.at[position * owned + i], send.at[position, i], recv.at[position, i],
            member(position),
        )

    forward_set = (
        local_ref, group_ref, chain_ref, leave_ref, enter_ref, state_ref,
        up_send, up_recv, chain_send, chain_recv, down_send, down_recv,
    )
    backward_set = (
        blocal_ref, bgroup_ref, bchain_ref, bleave_ref, benter_ref, bstate_ref,
        bup_send, bup_recv, bchain_send, bchain_recv, bdown_send, bdown_recv,
    )

    def send_local(i, buffers):
        local, group, _, _, _, _, usend, urecv = buffers[:8]
        for d in (1, 2, 3):
            up_copy(local, group, usend, urecv, other(d), i).start()

    def marks_copy(position, slot):
        return remote(
            marks_ref.at[position], group_marks_ref.at[slot], marks_send.at[position], marks_recv.at[slot],
            member(position),
        )

    send_local(0, forward_set)
    for d in (1, 2, 3):
        marks_copy(other(d), c).start()

    @pl.when(s < nseq - 1)
    def _():
        ids_after().start()

    @pl.when(s > 0)
    def _():
        ids_before().start()

    def more_states(i, _):
        local_states(i)
        send_local(i, forward_set)
        return 0

    lax.fori_loop(1, owned, more_states, 0)

    columns = run.T
    grown = jnp.exp(run).T
    for h in range(heads):
        runc_ref[h] = jnp.broadcast_to(columns[:, h : h + 1], (tokens, width))
        grow_ref[h] = jnp.broadcast_to(grown[:, h : h + 1], (tokens, width))
    wide = jnp.concatenate([epc_ref[...]] * (tokens // width), axis=1)
    below = lax.broadcasted_iota(jnp.int32, (tokens, tokens), 0) >= lax.broadcasted_iota(
        jnp.int32, (tokens, tokens), 1
    )
    allow_ref[...] = jnp.where(below & (wide == ep_row), 0.0, BLOCKED)

    def chain_copy(buffers, i, slot, distance, sign):
        _, _, chain, _, enter, _, _, _, csend, crecv, _, _ = buffers
        return remote(
            enter.at[i], chain.at[slot, i], csend.at[distance - 1, i], crecv.at[slot, i],
            {"seq": s + sign * GROUP * distance},
        )

    def place(sign):
        return z if sign > 0 else groups - 1 - z

    def latter(sign):
        return lax.rem(place(sign), 2) == 1

    def send_total(i, sign, buffers):
        local, group, chain, leave, enter, state, usend, urecv, csend, crecv, dsend, drecv = buffers
        id_row = owned if sign > 0 else owned + 1
        for d in range(1, GROUP):
            up_arrival(local, group, usend, urecv, other(d), i).wait_recv()
        total_state = None
        for j in range(GROUP)[::sign]:
            factor = group_marks_ref[j, pl.ds(i, 1), :]
            mark = group_marks_ref[j, id_row : id_row + 1, :]
            if total_state is None:
                total_state = group[j, i]
                factors = factor
            else:
                total_state = total_state * jnp.where(mark == before, factor, 0.0) + group[j, i]
                factors = factors * factor
            before = mark
        enter[i, 0:width] = total_state
        enter[i, width:] = jnp.where(row == 0, factors, before)

        @pl.when(jnp.logical_not(latter(sign)))
        def _():
            chain_copy(buffers, i, 1, 1, sign).start()

    def receive_state(i, sign, buffers):
        chain = buffers[2]

        @pl.when(place(sign) < 2)
        def _():
            chain[0, i] = jnp.zeros((width + 8, width), F32)

        @pl.when(place(sign) >= 2)
        def _():
            chain_copy(buffers, i, 0, 1, -sign).wait_recv()

    def join_pair(i, sign, buffers):
        chain, enter = buffers[2], buffers[4]
        receive_state(i, sign, buffers)
        chain_copy(buffers, i, 1, 1, -sign).wait_recv()
        mark = chain[1, i, width + 1 : width + 2, :]
        factor = jnp.where(mark == chain[0, i, width + 1 : width + 2, :], chain[1, i, width : width + 1, :], 0.0)
        entering = chain[0, i, 0:width] * factor + chain[1, i, 0:width]
        chain[0, i, 0:width] = entering
        chain[0, i, width:] = jnp.broadcast_to(mark, (8, width))
        own = enter[i, width + 1 : width + 2, :]
        factor = jnp.where(own == mark, enter[i, width : width + 1, :], 0.0)
        enter[i, 0:width] = entering * factor + enter[i, 0:width]

    def send_next(i, sign, buffers):
        @pl.when(latter(sign) & (place(sign) < groups - 1))
        def _():
            join_pair(i, sign, buffers)
            chain_copy(buffers, i, 0, 1, sign).start()
            chain_copy(buffers, i, 0, 2, sign).start()

    def send_entering(i, sign, buffers):
        local, group, chain, leave, enter, state, usend, urecv, csend, crecv, dsend, drecv = buffers
        id_row = owned if sign > 0 else owned + 1

        @pl.when(place(sign) == groups - 1)
        def _():
            join_pair(i, sign, buffers)

        @pl.when(jnp.logical_not(latter(sign)))
        def _():
            receive_state(i, sign, buffers)

        carried = chain[0, i, 0:width]
        before = chain[0, i, width + 1 : width + 2, :]
        for n, j in enumerate(range(GROUP)[::sign]):
            leave[j, i] = carried
            if n < GROUP - 1:
                mark = group_marks_ref[j, id_row : id_row + 1, :]
                factor = jnp.where(mark == before, group_marks_ref[j, pl.ds(i, 1), :], 0.0)
                carried = carried * factor + group[j, i]
                before = mark
        for d in range(1, GROUP):
            down_copy(leave, state, dsend, drecv, other(d), i).start()
        state[c * owned + i] = leave[c, i]

    def state_arrival(i, buffers):
        _, _, _, leave, _, state, _, _, _, _, dsend, drecv = buffers
        for d in range(1, GROUP):
            down_arrival(leave, state, dsend, drecv, other(d), i).wait_recv()

    def settle(i, sign, buffers):
        local, group, _, leave, _, state, usend, urecv, _, _, dsend, drecv = buffers
        for d in range(1, GROUP):
            up_arrival(local, group, usend, urecv, other(d), i).wait_send()
            down_arrival(leave, state, dsend, drecv, other(d), i).wait_send()

        @pl.when(place(sign) < groups - 1)
        def _():
            chain_copy(buffers, i, 0, 1, sign).wait_send()

        @pl.when(latter(sign) & (place(sign) < groups - 1))
        def _():
            chain_copy(buffers, i, 0, 2, sign).wait_send()

    def scan(sign, buffers, part):
        def steps(i, _):
            send_total(i, sign, buffers)
            part(i)
            send_next(i, sign, buffers)

            @pl.when(i > 0)
            def _():
                send_entering(i - 1, sign, buffers)

            return 0

        lax.fori_loop(0, owned, steps, 0)
        send_entering(owned - 1, sign, buffers)

    def forward_part(i):
        for position in range(GROUP):
            h = position * owned + i
            runc = jnp.concatenate([runc_ref[h]] * (tokens // width), axis=1)
            decay = jnp.exp(runc - run_ref[pl.ds(h, 1), :] + allow_ref[...])
            decay_ref[h] = decay
            score = (product(q_ref[h], k_ref[h], 1, 1) * decay).astype(BF16)
            score_ref[h] = score
            att_ref[h] = product(score, v_ref[h], 1, 0)

    loads[2].wait()
    for d in (1, 2, 3):
        marks_copy(other(d), other(d)).wait()
    scan(1, forward_set, forward_part)

    @pl.when(s == 0)
    def _():
        prev_ref[...] = jnp.full_like(prev_ref, -1.0)

    @pl.when(s == nseq - 1)
    def _():
        next_ref[...] = jnp.full_like(next_ref, -1.0)

    @pl.when(s < nseq - 1)
    def _():
        ids_after().wait_send()
        ids_before().wait_recv()

    @pl.when(s > 0)
    def _():
        ids_before().wait_send()
        ids_after().wait_recv()

    prev_id = prev_ref[0:1, width - 1 : width]
    next_id = next_ref[0:1, 0:1]
    loads[3].wait()

    sums_ref[...] = jnp.zeros_like(sums_ref)

    def attend(i, _):
        state_arrival(i, forward_set)
        squares = sums_ref[0]
        crosses = sums_ref[1]
        for position in range(GROUP):
            h = position * owned + i
            carried = jnp.where(epc_ref[...] == prev_id, grow_ref[h], 0.0)
            low = state_ref[h].astype(BF16)
            att = att_ref[h] + product(q_ref[h], low, 1, 0) * carried
            att_ref[h] = att
            squares = squares + att * att
            crosses = crosses + go_ref[h].astype(F32) * att
        sums_ref[0] = squares
        sums_ref[1] = crosses
        return 0

    lax.fori_loop(0, owned, attend, 0)
    square = jnp.sum(sums_ref[0], axis=1, keepdims=True)
    cross = jnp.sum(sums_ref[1], axis=1, keepdims=True)
    first_half = lax.broadcasted_iota(jnp.int32, (tokens, width), 1) < width // 2
    stat_ref[...] = jnp.where(first_half, square, cross)

    def stat_copy(d, slot):
        return remote(
            stat_ref, other_ref.at[slot], stat_send.at[d - 1], stat_recv.at[slot], {"head": lax.rem(hd + d, nhead)}
        )

    for d in range(1, nhead):
        stat_copy(d, d - 1).start()
    for d in range(1, nhead):
        stat_copy(d, d - 1).wait()
    summed = stat_ref[...]
    for d in range(1, nhead):
        summed = summed + other_ref[d - 1]
    square = summed[:, 0:1]
    cross = summed[:, width // 2 : width // 2 + 1]
    mean_square = square / features + EPSILON
    inverse = lax.rsqrt(mean_square)
    norm_ref[...] = jnp.broadcast_to(inverse, (tokens, width))
    corr_ref[...] = jnp.broadcast_to(cross / (features * mean_square), (tokens, width))

    def back_local(i, _):
        for d in (1, 2, 3, 0):
            position = other(d)
            h = position * owned + i
            att = att_ref[h]
            normed_ref[h] = (att * norm_ref[...]).astype(BF16)
            grad = ((go_ref[h].astype(F32) - att * corr_ref[...]) * norm_ref[...]).astype(BF16)
            gattn_ref[h] = grad
            weight = jnp.where(epc_ref[...] == first_id, grow_ref[h], 0.0)
            decayed = (q_ref[h].astype(F32) * weight).astype(BF16)
            value = product(decayed, grad, 0, 0)
            if d == 0:
                bgroup_ref[c, i] = value
            else:
                blocal_ref[h] = value
                up_copy(blocal_ref, bgroup_ref, bup_send, bup_recv, position, i).start()
        return 0

    lax.fori_loop(0, owned, back_local, 0)
    normed_store = pltpu.make_async_copy(normed_ref, normed_out, out_sem.at[0])
    normed_store.start()

    def backward_part(i):
        for position in range(GROUP):
            h = position * owned + i
            grad = gattn_ref[h]
            grad_score = (product(grad, v_ref[h], 1, 1) * decay_ref[h]).astype(BF16)
            carried = jnp.where(epc_ref[...] == prev_id, grow_ref[h], 0.0)
            low = state_ref[h].astype(BF16)
            gq_ref[h] = (
                product(grad_score, k_ref[h], 1, 0) + product(grad, low, 1, 1) * carried
            ).astype(BF16)
            kin_ref[h] = product(grad_score, q_ref[h], 0, 0)
            vin_ref[h] = product(score_ref[h], grad, 0, 0)

    scan(-1, backward_set, backward_part)
    gq_store = pltpu.make_async_copy(gq_ref, gq_out, out_sem.at[1])
    gq_store.start()

    def stores(h):
        return (
            pltpu.make_async_copy(gk_ref.at[h], gk_out.at[h], gk_sem.at[h]),
            pltpu.make_async_copy(gv_ref.at[h], gv_out.at[h], gv_sem.at[h]),
        )

    def finish(i, _):
        state_arrival(i, backward_set)
        for position in range(GROUP):
            h = position * owned + i
            trailing = jnp.where(epc_ref[...] == next_id, fall_ref[h], 0.0)
            low = bstate_ref[h].astype(BF16)
            gk_ref[h] = (kin_ref[h] + product(v_ref[h], low, 1, 1) * trailing).astype(BF16)
            gv_ref[h] = (vin_ref[h] + product(k_ref[h], low, 1, 0) * trailing).astype(BF16)
            for store in stores(h):
                store.start()
        return 0

    lax.fori_loop(0, owned, finish, 0)

    def settle_all(i, _):
        settle(i, 1, forward_set)
        settle(i, -1, backward_set)
        for position in range(GROUP):
            for store in stores(position * owned + i):
                store.wait()
        return 0

    lax.fori_loop(0, owned, settle_all, 0)
    normed_store.wait()
    gq_store.wait()


def hand_over(*refs):
    sources, targets, held, in_sem, out_sem = refs[:4], refs[4:8], refs[8], refs[9], refs[10]
    pairs = []
    for n in range(len(sources)):
        heads = sources[n].shape[0]
        for part in range(2):
            rows = pl.ds(part * heads // 2, heads // 2)
            slot = held.at[n, rows]
            pairs.append((
                pltpu.make_async_copy(sources[n].at[rows], slot, in_sem.at[n, part]),
                pltpu.make_async_copy(slot, targets[n].at[rows], out_sem.at[n, part]),
            ))
    for load, _ in pairs:
        load.start()
    for load, store in pairs:
        load.wait()
        store.start()
    for _, store in pairs:
        store.wait()


def per_device(nseq, nhead, query_rows, key_rows, value_rows, log_gate, episode, grad_out):
    heads, tokens, width = query_rows.shape
    owned = heads // GROUP
    padded = -(-heads // 8) * 8
    if padded != heads:
        log_gate = jnp.pad(log_gate, ((0, padded - heads), (0, 0)))
    vmem = pl.BlockSpec(memory_space=pltpu.VMEM)
    outside = pl.BlockSpec(memory_space=pl.ANY)
    rows = jax.ShapeDtypeStruct(query_rows.shape, BF16)
    block = (heads, tokens, width)
    state_set = [
        pltpu.VMEM((heads, width, width), F32),
        pltpu.VMEM((GROUP, owned, width, width), F32),
        pltpu.VMEM((2, owned, width + 8, width), F32),
        pltpu.VMEM((GROUP, owned, width, width), F32),
        pltpu.VMEM((owned, width + 8, width), F32),
        pltpu.VMEM((heads, width, width), F32),
    ]
    sem_set = [
        pltpu.SemaphoreType.DMA((GROUP, owned)),
        pltpu.SemaphoreType.DMA((GROUP, owned)),
        pltpu.SemaphoreType.DMA((2, owned)),
        pltpu.SemaphoreType.DMA((2, owned)),
        pltpu.SemaphoreType.DMA((GROUP, owned)),
        pltpu.SemaphoreType.DMA((GROUP, owned)),
    ]
    others = max(nhead - 1, 1)
    results = pl.pallas_call(
        functools.partial(kernel, nseq, nhead, float(heads * nhead * width)),
        out_shape=[rows] * 4,
        in_specs=[outside, outside, outside, vmem, vmem, outside],
        out_specs=[outside] * 4,
        scratch_shapes=[
            *[pltpu.VMEM(block, BF16)] * 8,
            pltpu.VMEM((padded, tokens), F32),
            pltpu.VMEM(block, F32),
            pltpu.VMEM(block, F32),
            pltpu.VMEM(block, F32),
            pltpu.VMEM((padded, width), F32),
            pltpu.VMEM((tokens, tokens), F32),
            pltpu.VMEM((tokens, width), F32),
            pltpu.VMEM((heads, tokens, tokens), F32),
            pltpu.VMEM((heads, tokens, tokens), BF16),
            pltpu.VMEM(block, F32),
            pltpu.VMEM(block, BF16),
            pltpu.VMEM(block, F32),
            pltpu.VMEM(block, F32),
            pltpu.VMEM((2, tokens, width), F32),
            pltpu.VMEM((tokens, width), F32),
            pltpu.VMEM((others, tokens, width), F32),
            pltpu.VMEM((tokens, width), F32),
            pltpu.VMEM((tokens, width), F32),
            pltpu.VMEM((8, width), F32),
            pltpu.VMEM((8, width), F32),
            pltpu.VMEM((8, width), F32),
            pltpu.VMEM((GROUP, 8, width), F32),
            pltpu.VMEM((GROUP, 8, width), F32),
            *state_set,
            *state_set,
            pltpu.SemaphoreType.DMA((GROUP,)),
            pltpu.SemaphoreType.DMA((GROUP,)),
            pltpu.SemaphoreType.DMA((4,)),
            pltpu.SemaphoreType.DMA((2,)),
            pltpu.SemaphoreType.DMA((heads,)),
            pltpu.SemaphoreType.DMA((heads,)),
            pltpu.SemaphoreType.DMA((2,)),
            pltpu.SemaphoreType.DMA((2,)),
            pltpu.SemaphoreType.DMA((others,)),
            pltpu.SemaphoreType.DMA((others,)),
            *sem_set,
            *sem_set,
        ],
        compiler_params=pltpu.CompilerParams(
            collective_id=0, has_side_effects=True, vmem_limit_bytes=56 * MIB
        ),
        cost_estimate=pl.CostEstimate(
            flops=heads * tokens * tokens * width * 18, bytes_accessed=heads * tokens * width * 16,
            transcendentals=heads * tokens * tokens,
        ),
    )(query_rows, key_rows, value_rows, log_gate, episode.reshape(1, tokens), grad_out)
    return pl.pallas_call(
        hand_over,
        out_shape=[rows] * 4,
        in_specs=[outside] * 4,
        out_specs=[outside] * 4,
        scratch_shapes=[
            pltpu.VMEM((4, *block), BF16),
            pltpu.SemaphoreType.DMA((4, 2)),
            pltpu.SemaphoreType.DMA((4, 2)),
        ],
        compiler_params=pltpu.CompilerParams(vmem_limit_bytes=56 * MIB),
    )(*results)


def solution(mesh):
    rows = P("head", "seq", None)
    return jax.shard_map(
        functools.partial(per_device, mesh.shape["seq"], mesh.shape["head"]),
        mesh=mesh,
        in_specs=(rows, rows, rows, P("head", "seq"), P("seq"), rows),
        out_specs=(rows, rows, rows, rows),
        check_vma=False,
    )
```
